32 devices in a mesh: gx: 8 (over y, x, core), col: 4 (over z).
Axes of the slice: x: 2, y: 2, z: 4, core: 2. Of those that a mesh axis runs over, the one named last changes fastest.
Arguments:
- field: bfloat16 [32, 16, 128, 256], P('col', 'gx'), may hold values from -6 to 6
- kernel: bfloat16 [64, 32, 3, 3, 3], replicated, may hold values from -0.21875 to 0.21875
- bias: float32 [64], P('col'), may hold values from -3 to 3
- cotangent: bfloat16 [64, 8, 64, 128], P('col', 'gx'), may hold values from -6 to 6
Outputs:
- out_act: bfloat16 [64, 8, 64, 128], P('col', 'gx')
- in_grad: bfloat16 [32, 16, 128, 256], P('col', 'gx')
The draws below stay inside these ranges and needn't reach their ends.
All inputs are finite; a program needn't handle non-finite values.
Results may differ from the reference program's by a relative error of at most 0.014.
Values may be sent and summed in bfloat16 or wider, within the bound.
No kernel may reach another device: no remote copies, remote signals or barrier semaphores. Data moves between devices by JAX's collectives and lax.ppermute only.
A program may use at most 128 MiB of HBM per device.

```python
import jax
import jax.numpy as jnp
from jax import lax

CIN = 32
COUT = 64
Y = 128
Z = 256
X = 16


def steps_of(stream_key, extent, pieces, low, high):
    factor_of, own = 1.0, jax.random.fold_in(stream_key, 6)
    for dim, shards_of in pieces:
        draws = jnp.exp(jax.random.uniform(jax.random.fold_in(own, dim), (shards_of,), jnp.float32, low / len(pieces), high / len(pieces)))
        factor_of = factor_of * jnp.repeat(draws, extent[dim] // shards_of).reshape([-1 if axis == dim else 1 for axis in range(len(extent))])
    return factor_of


def bell_draw(stream_key, extent, width, reach, shards=(), kind=jnp.bfloat16):
    gain = steps_of(stream_key, extent, shards, -0.22, 0.18) if shards else 1.0
    values = jax.random.normal(stream_key, extent, jnp.float32) * width * gain
    return jnp.minimum(jnp.maximum(values, -reach), reach).astype(kind)


def setup_inputs(seed: int = 0) -> dict:
    splits = jax.random.split(jax.random.key(seed), 5)
    field = bell_draw(splits[0], (CIN, X, Y, Z), 1.0, 6.0, ((0, 4), (1, 8)))
    kernel = bell_draw(splits[1], (COUT, CIN, 3, 3, 3), (CIN * 27) ** -0.5, 0.21875)
    bias = bell_draw(splits[2], (COUT,), 0.5, 3.0, ((0, 4),), jnp.float32)
    cotangent = bell_draw(splits[3], (COUT, X // 2, Y // 2, Z // 2), 1.0, 6.0, ((0, 4), (1, 8)))
    return dict(field=field, kernel=kernel, bias=bias, cotangent=cotangent)


def periodic_conv(values, kernel_wide):
    padded = jnp.pad(values, ((0, 0), (1, 1), (1, 1), (1, 1)), mode='wrap')
    result = lax.conv_general_dilated(padded[None], kernel_wide, (2, 2, 2), 'VALID', dimension_numbers=('NCDHW', 'OIDHW', 'NCDHW'), precision=lax.Precision.HIGHEST)
    return result[0]

def reference(field, kernel, bias, cotangent):
    kernel_wide = kernel.astype(jnp.float32)
    field_wide = field.astype(jnp.float32)
    pre = periodic_conv(field_wide, kernel_wide) + bias.astype(jnp.float32)[:, None, None, None]
    out_act = (0.3 * pre + 0.7 * jax.nn.softplus(pre)).astype(jnp.bfloat16)
    masked = (cotangent.astype(jnp.float32) * (0.3 + 0.7 * jax.nn.sigmoid(pre))).astype(jnp.bfloat16)

    def forward_map(values):
        return periodic_conv(values, kernel_wide)
    _, pullback = jax.vjp(forward_map, field_wide)
    in_grad, = pullback(masked.astype(jnp.float32))
    return (out_act, in_grad.astype(jnp.bfloat16))
```

```python
import functools

import jax
import jax.numpy as jnp
from jax import lax
from jax.experimental import pallas as pl
from jax.experimental.pallas import tpu as pltpu
from jax.sharding import PartitionSpec as P

F32 = jnp.float32
BF16 = jnp.bfloat16
LANES = 128
ROWS = 16
PARAMS = pltpu.CompilerParams(vmem_limit_bytes=24 * 1024 * 1024)


def shifted(block, axis, distance):
    count = lax.axis_size(axis)
    return lax.ppermute(block, axis, [(i, (i + distance) % count) for i in range(count)])


def one_hot(shape, rule):
    rows = lax.broadcasted_iota(jnp.int32, shape, 0)
    cols = lax.broadcasted_iota(jnp.int32, shape, 1)
    return jnp.where(rule(rows, cols), 1.0, 0.0).astype(BF16)


def dot(left, right):
    return jnp.dot(left, right, preferred_element_type=F32)


def fill_taps(plane_of, chans, span_y, span_z, taps_ref, first_row):
    half_z = span_z // 2
    size = chans * ROWS
    swap = one_hot((size, size), lambda r, c: c == (r % chans) * ROWS + r // chans)
    split = one_hot(
        (span_z, 3 * half_z),
        lambda z, m: z == (2 * (m % half_z) + m // half_z + span_z - 1) % span_z,
    )
    pair = 2 * chans
    for block in range(span_y // ROWS):
        swapped = dot(swap, plane_of(block)).astype(BF16)
        tapped = dot(swapped, split).astype(BF16)
        for j in range(ROWS // 2):
            half_y = block * (ROWS // 2) + j
            for tap in range(3):
                tile = tapped[j * pair : (j + 1) * pair, tap * half_z : (tap + 1) * half_z]
                row = first_row + tap * pair
                lane = (1 + half_y) * half_z
                taps_ref[row : row + pair, lane : lane + half_z] = tile
                if half_y == span_y // 2 - 1:
                    taps_ref[row : row + pair, 0:half_z] = tile


def tap_sums(weights, taps_ref, lane, width, half_z):
    before = taps_ref[:, lane : lane + width]
    here = taps_ref[:, lane + half_z : lane + half_z + width]
    return dot(weights, jnp.concatenate([before, here], axis=0))


def local_kernel(field_ref, weight_ref, acc_ref, taps_ref):
    chans, planes, span_y, span_z = field_ref.shape
    half_z = span_z // 2
    for plane in range(planes):
        def plane_of(block, plane=plane):
            rows = field_ref[:, plane, block * ROWS : (block + 1) * ROWS, :]
            return rows.reshape(chans * ROWS, span_z)

        fill_taps(plane_of, chans, span_y, span_z, taps_ref, plane * 6 * chans)
    weights = weight_ref[...]
    width = 8 * half_z
    for step in range(span_y // 16):
        lane = step * width
        acc_ref[:, lane : lane + width] = tap_sums(weights, taps_ref, lane, width, half_z)


def halo_kernel(halo_ref, weight_ref, acc_ref, parts_ref, taps_ref):
    chans, span_y, span_z = halo_ref.shape
    half_z = span_z // 2

    def plane_of(block):
        return halo_ref[:, block * ROWS : (block + 1) * ROWS, :].reshape(chans * ROWS, span_z)

    fill_taps(plane_of, chans, span_y, span_z, taps_ref, 0)
    weights = weight_ref[...]
    peers, _, rows, _ = parts_ref.shape
    width = 8 * half_z
    for step in range(span_y // 16):
        lane = step * width
        sums = acc_ref[:, lane : lane + width] + tap_sums(weights, taps_ref, lane, width, half_z)
        sums = sums.astype(BF16)
        for j in range(8):
            for peer in range(peers):
                parts_ref[peer, step * 8 + j] = sums[
                    peer * rows : (peer + 1) * rows, j * half_z : (j + 1) * half_z
                ]


def act_kernel(*refs):
    *part_refs, bias_ref, cot_ref, out_ref, masked_ref = refs
    pre = bias_ref[...] + functools.reduce(
        lambda a, b: a + b, [ref[...].astype(F32) for ref in part_refs]
    )
    small = jnp.exp(-jnp.abs(pre))
    soft = jnp.maximum(pre, 0.0) + jnp.log(1.0 + small)
    out_ref[...] = (0.3 * pre + 0.7 * soft).astype(BF16)
    gate = jnp.where(pre >= 0.0, 1.0, small) / (1.0 + small)
    masked_ref[...] = (cot_ref[...].astype(F32) * (0.3 + 0.7 * gate)).astype(BF16)


def grad_kernel(*refs):
    *piece_refs, weight_ref, grad_ref, held_ref = refs
    chans, _, span_y, span_z = grad_ref.shape
    half_y, half_z = span_y // 2, span_z // 2
    for index, ref in enumerate(piece_refs):
        row = index * ROWS
        for j in range(half_y):
            tile = ref[j]
            held_ref[row : row + ROWS, j * half_z : (j + 1) * half_z] = tile
            if j == 0:
                held_ref[row : row + ROWS, half_y * half_z :] = tile
    size = chans * ROWS
    swap = one_hot((size, size), lambda r, c: c == (r % ROWS) * chans + r // ROWS)
    weave = one_hot((span_z, span_z), lambda m, z: z == 2 * (m % half_z) + m // half_z)
    weights = weight_ref[...]
    pair = 2 * chans
    width = 8 * half_z
    for step in range(half_y // 8):
        lane = step * width
        here = held_ref[:, lane : lane + width]
        after = held_ref[:, lane + half_z : lane + half_z + width]
        sums = dot(weights, jnp.concatenate([here, after], axis=0))
        for parity_x in range(2):
            base = parity_x * 3 * pair
            rows = []
            for j in range(8):
                tile = sums[base : base + 3 * pair, j * half_z : (j + 1) * half_z]
                even = tile[:pair]
                odd = tile[pair : 2 * pair] + pltpu.roll(tile[2 * pair :], half_z - 1, 1)
                rows.append(jnp.concatenate([even.astype(BF16), odd.astype(BF16)], axis=1))
            swapped = dot(swap, jnp.concatenate(rows, axis=0)).astype(BF16)
            woven = dot(swapped, weave).astype(BF16)
            for chan in range(chans):
                grad_ref[chan, parity_x, step * ROWS : (step + 1) * ROWS, :] = woven[
                    chan * ROWS : (chan + 1) * ROWS
                ]


def forward_weights(own):
    peers, rows, cin = own.shape[:3]
    lead = jnp.pad(own, ((0, 0),) * 4 + ((1, 0), (0, 0)))
    lead = lead.reshape(*lead.shape[:4], 2, 2, 3)
    cols = jnp.transpose(lead, (0, 1, 4, 3, 6, 5, 2))
    local = cols[:, :, :, 1:].reshape(peers * rows, 2 * 2 * 3 * 2 * cin)
    halo = cols[:, :, :, :1].reshape(peers * rows, 2 * 1 * 3 * 2 * cin)
    return local, halo


def backward_weights(own):
    peers, rows, cin = own.shape[:3]
    none = jnp.zeros_like(own[:, :, :, 0])
    by_x = jnp.stack(
        [
            jnp.stack([own[:, :, :, 1], none]),
            jnp.stack([own[:, :, :, 2], own[:, :, :, 0]]),
        ]
    )
    none = jnp.zeros_like(by_x[..., 0, :])
    by_y = jnp.stack(
        [
            jnp.stack([by_x[..., 1, :], none]),
            jnp.stack([by_x[..., 2, :], by_x[..., 0, :]]),
        ]
    )
    by_z = jnp.stack([by_y[..., 1], by_y[..., 2], by_y[..., 0]])
    turned = jnp.transpose(by_z, (3, 0, 1, 7, 2, 4, 5, 6))
    return turned.reshape(2 * 3 * 2 * cin, 2 * 2 * peers * rows)


def on_device(field, kernel, bias, cotangent):
    peers = lax.axis_size("col")
    me = lax.axis_index("col")
    cin, planes, span_y, span_z = field.shape
    cout = bias.shape[0]
    half_y, half_z = span_y // 2, span_z // 2
    halo = shifted(field[:, planes - 1], "gx", 1)

    chans = -(-cin // 8) * 8
    rows = -(-cout // ROWS) * ROWS
    own = lax.dynamic_slice_in_dim(kernel, me * cin, cin, 1)
    own = own.reshape(peers, cout, cin, 3, 3, 3)
    twice = jnp.concatenate([own, own], axis=0)
    ahead = lax.dynamic_slice_in_dim(twice, me, peers, 0)
    behind = lax.dynamic_slice_in_dim(twice[::-1], peers - 1 - me, peers, 0)
    fill_w = ((0, 0), (0, rows - cout), (0, chans - cin), (0, 0), (0, 0), (0, 0))
    ahead, behind = jnp.pad(ahead, fill_w), jnp.pad(behind, fill_w)
    fill_c = (0, chans - cin)
    field_p = jnp.pad(field, (fill_c, (0, 0), (0, 0), (0, 0)))
    halo_p = jnp.pad(halo, (fill_c, (0, 0), (0, 0)))
    weights_local, weights_halo = forward_weights(ahead)

    total = peers * rows
    acc = pl.pallas_call(
        local_kernel,
        out_shape=jax.ShapeDtypeStruct((total, half_y * half_z), F32),
        scratch_shapes=[pltpu.VMEM((planes * 6 * chans, (1 + half_y) * half_z), BF16)],
        compiler_params=PARAMS,
        cost_estimate=pl.CostEstimate(
            flops=2 * total * 24 * chans * half_y * half_z, bytes_accessed=1 << 22, transcendentals=0
        ),
        name="local_planes",
    )(field_p, weights_local)
    parts = pl.pallas_call(
        halo_kernel,
        out_shape=jax.ShapeDtypeStruct((peers, half_y, rows, half_z), BF16),
        scratch_shapes=[pltpu.VMEM((6 * chans, (1 + half_y) * half_z), BF16)],
        compiler_params=PARAMS,
        cost_estimate=pl.CostEstimate(
            flops=2 * total * 12 * chans * half_y * half_z, bytes_accessed=1 << 22, transcendentals=0
        ),
        name="halo_plane",
    )(halo_p, weights_halo, acc)

    arrived = [parts[0]] + [shifted(parts[r], "col", r) for r in range(1, peers)]
    fill_o = (0, rows - cout)
    bias_p = jnp.broadcast_to(jnp.pad(bias, fill_o)[None, :, None], (1, rows, half_z))
    cot_p = jnp.pad(jnp.transpose(cotangent[:, 0], (1, 0, 2)), ((0, 0), fill_o, (0, 0)))
    shape = jax.ShapeDtypeStruct((half_y, rows, half_z), BF16)
    out, masked = pl.pallas_call(
        act_kernel,
        out_shape=(shape, shape),
        compiler_params=PARAMS,
        cost_estimate=pl.CostEstimate(
            flops=20 * half_y * rows * half_z, bytes_accessed=1 << 21, transcendentals=3 * half_y * rows * half_z
        ),
        name="activation",
    )(*arrived, bias_p, cot_p)
    out_act = jnp.transpose(out[:, :cout], (1, 0, 2))[:, None]

    gathered = [masked] + [shifted(masked, "col", r) for r in range(1, peers)]
    above = [shifted(piece, "gx", -1) for piece in gathered]
    weights_back = backward_weights(behind)
    in_grad = pl.pallas_call(
        grad_kernel,
        out_shape=jax.ShapeDtypeStruct((chans, planes, span_y, span_z), BF16),
        scratch_shapes=[pltpu.VMEM((2 * total, (1 + half_y) * half_z), BF16)],
        compiler_params=PARAMS,
        cost_estimate=pl.CostEstimate(
            flops=2 * 4 * total * 12 * chans * half_y * half_z, bytes_accessed=1 << 22, transcendentals=0
        ),
        name="transposed_taps",
    )(*gathered, *above, weights_back)
    return out_act, in_grad[:cin]


def solution(mesh):
    in_specs = (P("col", "gx", None, None), P(), P("col"), P("col", "gx", None, None))
    out_specs = (P("col", "gx", None, None), P("col", "gx", None, None))
    return jax.shard_map(
        on_device, mesh=mesh, in_specs=in_specs, out_specs=out_specs, check_vma=False
    )
```

```python
import functools

import jax
import jax.numpy as jnp
from jax import lax
from jax.experimental import pallas as pl
from jax.experimental.pallas import tpu as pltpu
from jax.sharding import PartitionSpec as P

F32 = jnp.float32
BF16 = jnp.bfloat16
LANES = 128
ROWS = 16
PARAMS = pltpu.CompilerParams(vmem_limit_bytes=24 * 1024 * 1024)


def shifted(block, axis, distance):
    count = lax.axis_size(axis)
    return lax.ppermute(block, axis, [(i, (i + distance) % count) for i in range(count)])


def one_hot(shape, rule):
    rows = lax.broadcasted_iota(jnp.int32, shape, 0)
    cols = lax.broadcasted_iota(jnp.int32, shape, 1)
    return jnp.where(rule(rows, cols), 1.0, 0.0).astype(BF16)


def dot(left, right):
    return jnp.dot(left, right, preferred_element_type=F32)


def fill_taps(blocks, chans, span_z, taps_ref, first_row):
    half_z = span_z // 2
    size = chans * ROWS
    swap = one_hot((size, size), lambda r, c: c == (r % chans) * ROWS + r // chans)
    split = one_hot(
        (span_z, 3 * half_z),
        lambda z, m: z == (2 * (m % half_z) + m // half_z + span_z - 1) % span_z,
    )
    pair = 2 * chans
    for values, first, count, place in blocks:
        swapped = dot(swap, values()).astype(BF16)
        tapped = dot(swapped, split).astype(BF16)
        for j in range(count):
            for tap in range(3):
                row = first_row + tap * pair
                lane = (place + j) * half_z
                taps_ref[row : row + pair, lane : lane + half_z] = tapped[
                    (first + j) * pair : (first + j + 1) * pair, tap * half_z : (tap + 1) * half_z
                ]


def rows_of(ref, index, block):
    def values():
        rows = ref[(slice(None), *index, slice(block * ROWS, (block + 1) * ROWS))]
        return rows.reshape(rows.shape[0] * ROWS, rows.shape[-1])

    return values


def tap_sums(weights, taps_ref, lane, width, half_z):
    before = taps_ref[:, lane : lane + width]
    here = taps_ref[:, lane + half_z : lane + half_z + width]
    return dot(weights, jnp.concatenate([before, here], axis=0))


def local_kernel(field_ref, weight_ref, acc_ref, taps_ref):
    chans, planes, span_y, span_z = field_ref.shape
    half_z = span_z // 2
    count = span_y // ROWS
    for plane in range(planes):
        blocks = [(rows_of(field_ref, (plane,), b), 0, 8, 1 + 8 * b) for b in range(count)]
        blocks.append((rows_of(field_ref, (plane,), count - 1), 7, 1, 0))
        fill_taps(blocks, chans, span_z, taps_ref, plane * 6 * chans)
    weights = weight_ref[...]
    width = 8 * half_z
    for step in range(count):
        lane = step * width
        acc_ref[:, lane : lane + width] = tap_sums(weights, taps_ref, lane, width, half_z)


def halo_kernel(part, *refs):
    halo_refs, (weight_ref, acc_ref), part_refs, taps_ref = (
        refs[: part + 1],
        refs[part + 1 : part + 3],
        refs[part + 3 : -1],
        refs[-1],
    )
    chans, _, span_z = halo_refs[0].shape
    half_z = span_z // 2
    lower = halo_refs[0].shape[1] // ROWS - 1
    if part == 0:
        blocks = [(rows_of(halo_refs[0], (), 0), 7, 1, 0)]
        blocks += [(rows_of(halo_refs[0], (), 1 + b), 0, 8, 1 + 8 * b) for b in range(lower)]
    else:
        upper = halo_refs[1].shape[1] // ROWS
        blocks = [(rows_of(halo_refs[0], (), lower), 7, 1, 0)]
        blocks += [(rows_of(halo_refs[1], (), b), 0, 8, 1 + 8 * b) for b in range(upper)]
        blocks += [(rows_of(halo_refs[0], (), 0), 0, 8, 1 + 8 * upper)]
    fill_taps(blocks, chans, span_z, taps_ref, 0)
    weights = weight_ref[...]
    count, rows, _ = part_refs[0].shape
    width = 8 * half_z
    base = part * (acc_ref.shape[1] - count * half_z)
    for step in range(count // 8):
        lane = step * width
        sums = acc_ref[:, base + lane : base + lane + width]
        sums = (sums + tap_sums(weights, taps_ref, lane, width, half_z)).astype(BF16)
        for j in range(8):
            for peer, ref in enumerate(part_refs):
                ref[step * 8 + j] = sums[
                    peer * rows : (peer + 1) * rows, j * half_z : (j + 1) * half_z
                ]


def add_kernel(one_ref, two_ref, sum_ref):
    sum_ref[...] = (one_ref[...].astype(F32) + two_ref[...].astype(F32)).astype(BF16)


def act_kernel(*refs):
    *part_refs, bias_ref, cot_ref, out_ref, masked_ref = refs
    pre = bias_ref[...] + functools.reduce(
        lambda a, b: a + b, [ref[...].astype(F32) for ref in part_refs]
    )
    small = jnp.exp(-jnp.abs(pre))
    soft = jnp.maximum(pre, 0.0) + jnp.log(1.0 + small)
    out_ref[...] = (0.3 * pre + 0.7 * soft).astype(BF16)
    gate = jnp.where(pre >= 0.0, 1.0, small) / (1.0 + small)
    masked_ref[...] = (cot_ref[...].astype(F32) * (0.3 + 0.7 * gate)).astype(BF16)


def grad_blocks(held_ref, weights, blocks, chans, span_z, store):
    half_z = span_z // 2
    size = chans * ROWS
    swap = one_hot((size, size), lambda r, c: c == (r % ROWS) * chans + r // ROWS)
    weave = one_hot((span_z, span_z), lambda m, z: z == 2 * (m % half_z) + m // half_z)
    pair = 2 * chans
    width = 8 * half_z
    for step in range(blocks):
        lane = step * width
        here = held_ref[:, lane : lane + width]
        after = held_ref[:, lane + half_z : lane + half_z + width]
        sums = dot(weights, jnp.concatenate([here, after], axis=0))
        for parity_x in range(2):
            base = parity_x * 3 * pair
            rows = []
            for j in range(8):
                tile = sums[base : base + 3 * pair, j * half_z : (j + 1) * half_z]
                even = tile[:pair]
                odd = tile[pair : 2 * pair] + pltpu.roll(tile[2 * pair :], half_z - 1, 1)
                rows.append(jnp.concatenate([even.astype(BF16), odd.astype(BF16)], axis=1))
            swapped = dot(swap, jnp.concatenate(rows, axis=0)).astype(BF16)
            woven = dot(swapped, weave).astype(BF16)
            for chan in range(chans):
                store(chan, parity_x, step, woven[chan * ROWS : (chan + 1) * ROWS])


def lower_grad_kernel(*refs):
    *piece_refs, weight_ref, grad_ref, held_ref = refs
    chans, _, span_y, span_z = grad_ref.shape
    half_z = span_z // 2
    for index, ref in enumerate(piece_refs):
        row = index * ROWS
        for j in range(span_y // 2 + 1):
            held_ref[row : row + ROWS, j * half_z : (j + 1) * half_z] = ref[j]

    def store(chan, parity_x, step, values):
        grad_ref[chan, parity_x, step * ROWS : (step + 1) * ROWS, :] = values

    grad_blocks(held_ref, weight_ref[...], span_y // ROWS, chans, span_z, store)


def upper_grad_kernel(*refs):
    *piece_refs, weight_ref, lower_ref, grad_ref, held_ref = refs
    chans, _, span_y, span_z = grad_ref.shape
    half_z = span_z // 2
    done = lower_ref.shape[2]
    grad_ref[:, :, :done, :] = lower_ref[...]
    pieces = len(piece_refs) // 2
    for index in range(pieces):
        row = index * ROWS
        low, high = piece_refs[index], piece_refs[pieces + index]
        count = low.shape[0]
        tiles = [(low, j) for j in range(done // 2, count)]
        tiles += [(high, j) for j in range(high.shape[0])] + [(low, 0)]
        for place, (ref, j) in enumerate(tiles):
            held_ref[row : row + ROWS, place * half_z : (place + 1) * half_z] = ref[j]

    def store(chan, parity_x, step, values):
        first = done + step * ROWS
        grad_ref[chan, parity_x, first : first + ROWS, :] = values

    grad_blocks(held_ref, weight_ref[...], (span_y - done) // ROWS, chans, span_z, store)


def forward_weights(own):
    peers, rows, cin = own.shape[:3]
    lead = jnp.pad(own, ((0, 0),) * 4 + ((1, 0), (0, 0)))
    lead = lead.reshape(*lead.shape[:4], 2, 2, 3)
    cols = jnp.transpose(lead, (0, 1, 4, 3, 6, 5, 2))
    local = cols[:, :, :, 1:].reshape(peers * rows, 2 * 2 * 3 * 2 * cin)
    halo = cols[:, :, :, :1].reshape(peers * rows, 2 * 1 * 3 * 2 * cin)
    return local, halo


def backward_weights(own):
    peers, rows, cin = own.shape[:3]
    none = jnp.zeros_like(own[:, :, :, 0])
    by_x = jnp.stack(
        [
            jnp.stack([own[:, :, :, 1], none]),
            jnp.stack([own[:, :, :, 2], own[:, :, :, 0]]),
        ]
    )
    none = jnp.zeros_like(by_x[..., 0, :])
    by_y = jnp.stack(
        [
            jnp.stack([by_x[..., 1, :], none]),
            jnp.stack([by_x[..., 2, :], by_x[..., 0, :]]),
        ]
    )
    by_z = jnp.stack([by_y[..., 1], by_y[..., 2], by_y[..., 0]])
    turned = jnp.transpose(by_z, (3, 0, 1, 7, 2, 4, 5, 6))
    return turned.reshape(2 * 3 * 2 * cin, 2 * 2 * peers * rows)


def call(kernel, name, out_shape, args, scratch=(), flops=0, bytes_accessed=1 << 20, transcendentals=0):
    return pl.pallas_call(
        kernel,
        out_shape=out_shape,
        scratch_shapes=list(scratch),
        compiler_params=PARAMS,
        cost_estimate=pl.CostEstimate(
            flops=flops, bytes_accessed=bytes_accessed, transcendentals=transcendentals
        ),
        name=name,
    )(*args)


def on_device(field, kernel, bias, cotangent):
    peers = lax.axis_size("col")
    me = lax.axis_index("col")
    quarter = peers // 4
    cin, planes, span_y, span_z = field.shape
    cout = bias.shape[0]
    half_y, half_z = span_y // 2, span_z // 2
    mid = span_y // 2
    last = span_y - ROWS
    plane = field[:, planes - 1]
    halos = [
        shifted(jnp.concatenate([plane[:, last:], plane[:, :mid]], axis=1), "gx", 1),
        shifted(plane[:, mid:last], "gx", 1),
    ]

    chans = -(-cin // 8) * 8
    rows = -(-cout // ROWS) * ROWS
    own = lax.dynamic_slice_in_dim(kernel, me * cin, cin, 1)
    own = own.reshape(peers, cout, cin, 3, 3, 3)
    twice = jnp.concatenate([own, own], axis=0)
    ahead = lax.dynamic_slice_in_dim(twice, me, peers, 0)
    behind = lax.dynamic_slice_in_dim(twice[::-1], peers - 1 - me, peers, 0)
    fill_w = ((0, 0), (0, rows - cout), (0, chans - cin), (0, 0), (0, 0), (0, 0))
    ahead, behind = jnp.pad(ahead, fill_w), jnp.pad(behind, fill_w)
    fill_c = (0, chans - cin)
    field_p = jnp.pad(field, (fill_c, (0, 0), (0, 0), (0, 0)))
    halos = [jnp.pad(halo, (fill_c, (0, 0), (0, 0))) for halo in halos]
    weights_local, weights_halo = forward_weights(ahead)

    total = peers * rows
    points = half_y * half_z
    acc = call(
        local_kernel,
        "local_planes",
        jax.ShapeDtypeStruct((total, points), F32),
        (field_p, weights_local),
        [pltpu.VMEM((planes * 6 * chans, (1 + half_y) * half_z), BF16)],
        flops=2 * total * 24 * chans * points,
        bytes_accessed=1 << 22,
    )
    half = half_y // 2
    piece = jax.ShapeDtypeStruct((half, rows, half_z), BF16)
    parts = [
        call(
            functools.partial(halo_kernel, part),
            "halo_plane",
            [piece] * peers,
            (*halos[: part + 1], weights_halo, acc),
            [pltpu.VMEM((6 * chans, (1 + half) * half_z), BF16)],
            flops=total * 12 * chans * points,
            bytes_accessed=1 << 21,
        )
        for part in range(2)
    ]

    steps = (quarter, peers - quarter)
    relayed = [shifted(parts[h][2 * quarter], "col", steps[h]) for h in range(2)]
    direct = [
        [shifted(parts[h][r], "col", r) for r in range(1, peers) if r not in (steps[h], 2 * quarter)]
        for h in range(2)
    ]
    joined = [call(add_kernel, "add", piece, (relayed[h], parts[h][steps[h]])) for h in range(2)]
    joined = [shifted(joined[h], "col", steps[h]) for h in range(2)]

    fill_o = (0, rows - cout)
    bias_p = jnp.broadcast_to(jnp.pad(bias, fill_o)[None, :, None], (1, rows, half_z))
    cot = jnp.pad(jnp.transpose(cotangent[:, 0], (1, 0, 2)), ((0, 0), fill_o, (0, 0)))
    acts = [
        call(
            act_kernel,
            "activation",
            (piece, piece),
            (parts[h][0], joined[h], *direct[h], bias_p, cot[h * half : (h + 1) * half]),
            transcendentals=3 * half * rows * half_z,
        )
        for h in range(2)
    ]
    out = jnp.concatenate([out for out, _ in acts], axis=0)
    out_act = jnp.transpose(out[:, :cout], (1, 0, 2))[:, None]

    masked = [masked for _, masked in acts]
    gathered = [{0: masked[h]} for h in range(2)]
    for h in range(2):
        for r in range(1, peers):
            if r != 2 * quarter:
                gathered[h][r] = shifted(masked[h], "col", r)
    for h in range(2):
        gathered[h][2 * quarter] = shifted(gathered[h][steps[h]], "col", steps[h])
    gathered = [[gathered[h][r] for r in range(peers)] for h in range(2)]
    above = [[shifted(value, "gx", -1) for value in gathered[h]] for h in range(2)]
    weights_back = backward_weights(behind)
    done = span_y // 2 - ROWS
    lower = call(
        lower_grad_kernel,
        "lower_grad",
        jax.ShapeDtypeStruct((chans, planes, done, span_z), BF16),
        (*gathered[0], *above[0], weights_back),
        [pltpu.VMEM((2 * total, (1 + done // 2) * half_z), BF16)],
        flops=3 * total * 12 * chans * points,
    )
    in_grad = call(
        upper_grad_kernel,
        "upper_grad",
        jax.ShapeDtypeStruct((chans, planes, span_y, span_z), BF16),
        (*gathered[0], *above[0], *gathered[1], *above[1], weights_back, lower),
        [pltpu.VMEM((2 * total, (1 + (span_y - done) // 2) * half_z), BF16)],
        flops=5 * total * 12 * chans * points,
        bytes_accessed=1 << 21,
    )
    return out_act, in_grad[:cin]


def solution(mesh):
    in_specs = (P("col", "gx", None, None), P(), P("col"), P("col", "gx", None, None))
    out_specs = (P("col", "gx", None, None), P("col", "gx", None, None))
    return jax.shard_map(
        on_device, mesh=mesh, in_specs=in_specs, out_specs=out_specs, check_vma=False
    )
```

```python
import functools

import jax
import jax.numpy as jnp
from jax import lax
from jax.experimental import pallas as pl
from jax.experimental.pallas import tpu as pltpu
from jax.sharding import PartitionSpec as P

F32 = jnp.float32
BF16 = jnp.bfloat16
LANES = 128
ROWS = 16
PARAMS = pltpu.CompilerParams(vmem_limit_bytes=24 * 1024 * 1024)


OPT = dict(rs_relay=(1, 1), ag_relay=(1, 1), ag_tie=1, gx_merge=1, delay=1, lower=32, fold=1, tie_own=0, rs_tie=2, tie_act=1)


def ring_device(place, count):
    if not OPT["fold"]:
        return place
    return jnp.where(2 * place < count, 2 * place, 2 * (count - place) - 1)


def ring_place(device, count):
    if not OPT["fold"]:
        return device
    return jnp.where(device % 2 == 0, device // 2, count - (device + 1) // 2)


def shifted(block, axis, distance):
    count = lax.axis_size(axis)
    ring = list(range(count))
    if axis == "col" and OPT["fold"]:
        ring = ring[::2] + ring[1::2][::-1]
    return lax.ppermute(block, axis, [(ring[i], ring[(i + distance) % count]) for i in range(count)])


def one_hot(shape, rule):
    rows = lax.broadcasted_iota(jnp.int32, shape, 0)
    cols = lax.broadcasted_iota(jnp.int32, shape, 1)
    return jnp.where(rule(rows, cols), 1.0, 0.0).astype(BF16)


def dot(left, right):
    return jnp.dot(left, right, preferred_element_type=F32)


def fill_taps(blocks, chans, span_z, taps_ref, first_row):
    half_z = span_z // 2
    size = chans * ROWS
    swap = one_hot((size, size), lambda r, c: c == (r % chans) * ROWS + r // chans)
    split = one_hot(
        (span_z, 3 * half_z),
        lambda z, m: z == (2 * (m % half_z) + m // half_z + span_z - 1) % span_z,
    )
    pair = 2 * chans
    beside = jnp.concatenate([values() for values, _, _, _ in blocks], axis=1)
    swapped = dot(swap, beside).astype(BF16)
    below = [swapped[:, i * span_z : (i + 1) * span_z] for i in range(len(blocks))]
    tapped = dot(jnp.concatenate(below, axis=0), split).astype(BF16)
    for index, (_, first, count, place) in enumerate(blocks):
        for j in range(count):
            for tap in range(3):
                source = index * size + (first + j) * pair
                row = first_row + tap * pair
                lane = (place + j) * half_z
                taps_ref[row : row + pair, lane : lane + half_z] = tapped[
                    source : source + pair, tap * half_z : (tap + 1) * half_z
                ]


def rows_of(ref, index, block):
    def values():
        rows = ref[(slice(None), *index, slice(block * ROWS, (block + 1) * ROWS))]
        return rows.reshape(rows.shape[0] * ROWS, rows.shape[-1])

    return values


def tap_sums(weights, taps_ref, lane, width, half_z):
    before = taps_ref[:, lane : lane + width]
    here = taps_ref[:, lane + half_z : lane + half_z + width]
    return dot(weights, jnp.concatenate([before, here], axis=0))


def local_kernel(field_ref, weight_ref, acc_ref, taps_ref):
    chans, planes, span_y, span_z = field_ref.shape
    half_z = span_z // 2
    count = span_y // ROWS
    for plane in range(planes):
        blocks = [(rows_of(field_ref, (plane,), b), 0, 8, 1 + 8 * b) for b in range(count)]
        fill_taps(blocks, chans, span_z, taps_ref, plane * 6 * chans)
    taps_ref[:, :half_z] = taps_ref[:, count * 8 * half_z :]
    weights = weight_ref[...]
    width = 8 * half_z
    for step in range(count):
        lane = step * width
        acc_ref[:, lane : lane + width] = tap_sums(weights, taps_ref, lane, width, half_z)


def halo_kernel(counts, halo_ref, weight_ref, acc_ref, *refs):
    *part_refs, taps_ref = refs
    chans, span_y, span_z = halo_ref.shape
    half_z = span_z // 2
    blocks = [(rows_of(halo_ref, (), b), 0, 8, 1 + 8 * b) for b in range(span_y // ROWS)]
    fill_taps(blocks, chans, span_z, taps_ref, 0)
    taps_ref[:, :half_z] = taps_ref[:, span_y // 2 * half_z :]
    weights = weight_ref[...]
    peers = len(part_refs) // len(counts)
    rows = part_refs[0].shape[1]
    width = 8 * half_z
    for step in range(span_y // 16):
        lane = step * width
        sums = acc_ref[:, lane : lane + width]
        sums = (sums + tap_sums(weights, taps_ref, lane, width, half_z)).astype(BF16)
        part = int(step * 8 >= counts[0])
        first = step * 8 - part * counts[0]
        for j in range(8):
            for peer in range(peers):
                part_refs[part * peers + peer][first + j] = sums[
                    peer * rows : (peer + 1) * rows, j * half_z : (j + 1) * half_z
                ]


def add_kernel(one_ref, two_ref, sum_ref):
    sum_ref[...] = (one_ref[...].astype(F32) + two_ref[...].astype(F32)).astype(BF16)


def act_kernel(*refs):
    *part_refs, bias_ref, cot_ref, out_ref, masked_ref = refs
    pre = bias_ref[...] + functools.reduce(
        lambda a, b: a + b, [ref[...].astype(F32) for ref in part_refs]
    )
    small = jnp.exp(-jnp.abs(pre))
    soft = jnp.maximum(pre, 0.0) + jnp.log(1.0 + small)
    out_ref[...] = (0.3 * pre + 0.7 * soft).astype(BF16)
    gate = jnp.where(pre >= 0.0, 1.0, small) / (1.0 + small)
    masked_ref[...] = (cot_ref[...].astype(F32) * (0.3 + 0.7 * gate)).astype(BF16)


def grad_blocks(held_ref, weights, blocks, chans, span_z, store):
    half_z = span_z // 2
    size = chans * ROWS
    swap = one_hot((size, size), lambda r, c: c == (r % ROWS) * chans + r // ROWS)
    weave = one_hot((span_z, span_z), lambda m, z: z == 2 * (m % half_z) + m // half_z)
    pair = 2 * chans
    width = blocks * 8 * half_z
    here, after = held_ref[:, :width], held_ref[:, half_z : half_z + width]
    sums = dot(weights, jnp.concatenate([here, after], axis=0))
    beside = []
    for step in range(blocks):
        for parity_x in range(2):
            base = parity_x * 3 * pair
            rows = []
            for j in range(step * 8, step * 8 + 8):
                tile = sums[base : base + 3 * pair, j * half_z : (j + 1) * half_z]
                even = tile[:pair]
                odd = tile[pair : 2 * pair] + pltpu.roll(tile[2 * pair :], half_z - 1, 1)
                rows.append(jnp.concatenate([even.astype(BF16), odd.astype(BF16)], axis=1))
            beside.append(jnp.concatenate(rows, axis=0))
    swapped = dot(swap, jnp.concatenate(beside, axis=1)).astype(BF16)
    below = [swapped[:, i * span_z : (i + 1) * span_z] for i in range(2 * blocks)]
    woven = dot(jnp.concatenate(below, axis=0), weave).astype(BF16)
    for step in range(blocks):
        for parity_x in range(2):
            for chan in range(chans):
                first = (step * 2 + parity_x) * size + chan * ROWS
                store(chan, parity_x, step, woven[first : first + ROWS])


def lower_grad_kernel(pieces, *refs):
    *piece_refs, weight_ref, grad_ref, held_ref = refs
    chans, _, span_y, span_z = grad_ref.shape
    half_z = span_z // 2
    for index, ((number, first), _) in enumerate(pieces):
        row = index * ROWS
        for j in range(span_y // 2 + 1):
            held_ref[row : row + ROWS, j * half_z : (j + 1) * half_z] = piece_refs[number][first + j]

    def store(chan, parity_x, step, values):
        grad_ref[chan, parity_x, step * ROWS : (step + 1) * ROWS, :] = values

    grad_blocks(held_ref, weight_ref[...], span_y // ROWS, chans, span_z, store)


def upper_grad_kernel(pieces, counts, *refs):
    *piece_refs, weight_ref, lower_ref, grad_ref, held_ref = refs
    chans, _, span_y, span_z = grad_ref.shape
    half_z = span_z // 2
    done = lower_ref.shape[2]
    grad_ref[:, :, :done, :] = lower_ref[...]
    for index, ((low, low_first), (high, high_first)) in enumerate(pieces):
        row = index * ROWS
        tiles = [(low, low_first + j) for j in range(done // 2, counts[0])]
        tiles += [(high, high_first + j) for j in range(counts[1])] + [(low, low_first)]
        for place, (number, j) in enumerate(tiles):
            held_ref[row : row + ROWS, place * half_z : (place + 1) * half_z] = piece_refs[number][j]

    def store(chan, parity_x, step, values):
        first = done + step * ROWS
        grad_ref[chan, parity_x, first : first + ROWS, :] = values

    grad_blocks(held_ref, weight_ref[...], (span_y - done) // ROWS, chans, span_z, store)


def weights_kernel(peers, me_ref, own_ref, local_ref, halo_ref, back_ref):
    _, chans, total = own_ref.shape
    rows = total // peers
    place = ring_place(me_ref[0], peers)

    def tile(tap_x, tap_y, tap_z):
        return own_ref[(tap_x * 3 + tap_y) * 3 + tap_z].astype(F32)

    none = jnp.zeros((chans, total), F32)

    def ahead(r, c):
        return c == ring_device((place + r // rows) % peers, peers) * rows + r % rows

    pick = one_hot((total, total), ahead)
    for ref, taps_x in ((local_ref, (1, 2)), (halo_ref, (0,))):
        tiles = [
            none if tap_y < 0 else tile(tap_x, tap_y, tap_z)
            for taps_y in ((-1, 0), (1, 2))
            for tap_x in taps_x
            for tap_z in range(3)
            for tap_y in taps_y
        ]
        stack = jnp.concatenate(tiles, axis=0).astype(BF16)
        ref[...] = lax.dot_general(
            pick, stack, (((1,), (1,)), ((), ())), preferred_element_type=F32
        ).astype(BF16)

    back = jnp.zeros(back_ref.shape, F32)
    by_offset = ((1, 2), (-1, 0))
    for offset in range(2):
        for plane in range(2):
            tiles = [
                none if min(tap_x, tap_y) < 0 else tile(tap_x, tap_y, tap_z)
                for tap_x in by_offset[plane]
                for tap_z in (1, 2, 0)
                for tap_y in by_offset[offset]
            ]
            stack = jnp.concatenate(tiles, axis=0).astype(BF16)
            first = (offset * 2 + plane) * total

            def behind(r, c, first=first):
                c = c - first
                device = ring_device((place + peers - c // rows) % peers, peers)
                return (r == device * rows + c % rows) & (c >= 0) & (c < total)

            back = back + dot(stack, one_hot((total, 4 * total), behind))
    back_ref[...] = back.astype(BF16)


def call(kernel, name, out_shape, args, scratch=(), flops=0, bytes_accessed=1 << 20, transcendentals=0):
    return pl.pallas_call(
        kernel,
        out_shape=out_shape,
        scratch_shapes=list(scratch),
        compiler_params=PARAMS,
        cost_estimate=pl.CostEstimate(
            flops=flops, bytes_accessed=bytes_accessed, transcendentals=transcendentals
        ),
        name=name,
    )(*args)


def on_device(field, kernel, bias, cotangent):
    peers = lax.axis_size("col")
    me = lax.axis_index("col")
    quarter = peers // 4
    cin, planes, span_y, span_z = field.shape
    cout = bias.shape[0]
    half_y, half_z = span_y // 2, span_z // 2
    counts = (OPT["lower"], half_y - OPT["lower"])
    starts = (0, counts[0])
    mid = 2 * counts[0]
    halo = shifted(field[:, planes - 1], "gx", 1)

    chans = -(-cin // 8) * 8
    rows = -(-cout // ROWS) * ROWS
    total = peers * rows
    fill_c = (0, chans - cin)
    fill_o = (0, rows - cout)
    own = lax.dynamic_slice_in_dim(jnp.transpose(kernel, (2, 3, 4, 1, 0)), me * cin, cin, 3)
    own = own.reshape(27, cin, peers, cout)
    own = jnp.pad(own, ((0, 0), fill_c, (0, 0), fill_o)).reshape(27, chans, total)
    field_p = jnp.pad(field, (fill_c, (0, 0), (0, 0), (0, 0)))

    points = half_y * half_z
    vmem = pl.BlockSpec(memory_space=pltpu.VMEM)
    weights_local, weights_halo, weights_back = pl.pallas_call(
        functools.partial(weights_kernel, peers),
        out_shape=[
            jax.ShapeDtypeStruct((total, 24 * chans), BF16),
            jax.ShapeDtypeStruct((total, 12 * chans), BF16),
            jax.ShapeDtypeStruct((12 * chans, 4 * total), BF16),
        ],
        in_specs=[pl.BlockSpec(memory_space=pltpu.SMEM), vmem],
        out_specs=[vmem] * 3,
        compiler_params=PARAMS,
        cost_estimate=pl.CostEstimate(flops=1 << 27, bytes_accessed=1 << 19, transcendentals=0),
        name="weights",
    )(me.astype(jnp.int32).reshape(1), own)
    acc = call(
        local_kernel,
        "local_planes",
        jax.ShapeDtypeStruct((total, points), F32),
        (field_p, weights_local),
        [
            pltpu.VMEM((planes * 6 * chans, (1 + half_y) * half_z), BF16),
        ],
        flops=2 * total * 24 * chans * points,
        bytes_accessed=1 << 22,
    )
    halo = jnp.pad(halo, (fill_c, (0, 0), (0, 0)))
    shapes = [jax.ShapeDtypeStruct((count, rows, half_z), BF16) for count in counts]
    sums = call(
        functools.partial(halo_kernel, counts),
        "halo_plane",
        [shapes[part] for part in range(2) for _ in range(peers)],
        (halo, weights_halo, acc),
        [
            pltpu.VMEM((6 * chans, (1 + half_y) * half_z), BF16),
        ],
        flops=2 * total * 12 * chans * points,
        bytes_accessed=1 << 22,
    )
    parts = (sums[:peers], sums[peers:])

    far = 2 * quarter
    steps = (quarter, peers - quarter)
    arrived = [[parts[h][0]] for h in range(2)]
    relayed = [shifted(parts[h][far], "col", steps[h]) if OPT["rs_relay"][h] else None for h in range(2)]
    for h in range(2):
        for r in range(1, peers):
            if not OPT["rs_relay"][h] or r not in (steps[h], far):
                sent = parts[h][r]
                if h and OPT["rs_tie"] >= 2:
                    sent, relayed[0] = lax.optimization_barrier((sent, relayed[0]))
                arrived[h].append(shifted(sent, "col", r))
    for h in range(2):
        if OPT["rs_tie"] == 1 or (OPT["rs_tie"] >= 3 and h == 0):
            relayed[h], arrived[h] = lax.optimization_barrier((relayed[h], arrived[h]))
        if OPT["rs_relay"][h]:
            joined = call(add_kernel, "add", shapes[h], (relayed[h], parts[h][steps[h]]))
            arrived[h].append(shifted(joined, "col", steps[h]))

    bias_p = jnp.broadcast_to(jnp.pad(bias, fill_o)[None, :, None], (1, rows, half_z))
    cot = jnp.pad(jnp.transpose(cotangent[:, 0], (1, 0, 2)), ((0, 0), fill_o, (0, 0)))
    acts = []
    for h in range(2):
        if h and OPT['tie_act']:
            bias_p, acts[0] = lax.optimization_barrier((bias_p, acts[0]))
        acts.append(
            call(
                act_kernel,
                "activation",
                (shapes[h], shapes[h]),
                (*arrived[h], bias_p, cot[starts[h] : starts[h] + counts[h]]),
                transcendentals=3 * counts[h] * rows * half_z,
            )
        )
    out = jnp.concatenate([out for out, _ in acts], axis=0)
    out_act = jnp.transpose(out[:, :cout], (1, 0, 2))[:, None]

    masked = [masked for _, masked in acts]
    gathered = [{0: masked[h]} for h in range(2)]
    for h in range(2):
        for r in range(1, peers):
            if r != far or not OPT["ag_relay"][h]:
                gathered[h][r] = shifted(masked[h], "col", r)
    above = [{}, {}]
    arrays = []

    def spec(value, *at):
        arrays.append(value)
        return len(arrays) - 1

    if OPT["gx_merge"]:
        whole = shifted(jnp.concatenate(masked, axis=0), "gx", -1)
        number = spec(whole)
        for h in range(2):
            above[h][0] = (number, starts[h])
    else:
        for h in range(2):
            above[h][0] = (spec(shifted(masked[h], "gx", -1)), 0)
    for h in range(2):
        if OPT["ag_tie"]:
            gathered[h] = lax.optimization_barrier(gathered[h])
        if h == 1 and OPT["tie_own"]:
            gathered[1][steps[1]], whole = lax.optimization_barrier((gathered[1][steps[1]], arrays[0]))
            arrays[0] = whole
    for h in range(2):
        near = [r for r in range(1, peers) if r != far]
        if OPT["gx_merge"]:
            number = spec(shifted(jnp.concatenate([gathered[h][r] for r in near], axis=0), "gx", -1))
            for i, r in enumerate(near):
                above[h][r] = (number, i * counts[h])
        else:
            for r in near:
                above[h][r] = (spec(shifted(gathered[h][r], "gx", -1)), 0)
    for h in range(2):
        if OPT["ag_relay"][h]:
            gathered[h][far] = shifted(gathered[h][steps[h]], "col", steps[h])
        above[h][far] = (spec(shifted(gathered[h][far], "gx", -1)), 0)
    mine = [{r: (spec(gathered[h][r]), 0) for r in range(peers)} for h in range(2)]
    order = [[places[h][r] for h in range(2)] for places in (mine, above) for r in range(peers)]

    def grad_call(kernel, name, shape, used, extra, blocks):
        used = sorted(used)
        renamed = [[(used.index(n) if n in used else -1, at) for n, at in both] for both in order]
        return call(
            functools.partial(kernel, renamed),
            name,
            shape,
            (*[arrays[n] for n in used], weights_back, *extra),
            [
                pltpu.VMEM((2 * total, (1 + 8 * blocks) * half_z), BF16),
            ],
            flops=8 * total * 12 * chans * 8 * blocks * half_z,
        )

    done = mid - ROWS
    lower = grad_call(
        lower_grad_kernel,
        "lower_grad",
        jax.ShapeDtypeStruct((chans, planes, done, span_z), BF16),
        {both[0][0] for both in order},
        (),
        done // ROWS,
    )
    in_grad = grad_call(
        lambda pieces, *refs: upper_grad_kernel(pieces, counts, *refs),
        "upper_grad",
        jax.ShapeDtypeStruct((chans, planes, span_y, span_z), BF16),
        {n for both in order for n, _ in both},
        (lower,),
        (span_y - done) // ROWS,
    )
    return out_act, in_grad[:cin]


def solution(mesh):
    in_specs = (P("col", "gx", None, None), P(), P("col"), P("col", "gx", None, None))
    out_specs = (P("col", "gx", None, None), P("col", "gx", None, None))
    return jax.shard_map(
        on_device, mesh=mesh, in_specs=in_specs, out_specs=out_specs, check_vma=False
    )
```

```python
import functools

import jax
import jax.numpy as jnp
from jax import lax
from jax.experimental import pallas as pl
from jax.experimental.pallas import tpu as pltpu
from jax.sharding import PartitionSpec as P

F32 = jnp.float32
BF16 = jnp.bfloat16
LANES = 128
ROWS = 16
PARAMS = pltpu.CompilerParams(vmem_limit_bytes=24 * 1024 * 1024)


OPT = dict(rs_relay=(1, 1), ag_relay=(1, 1), ag_tie=2, gx_merge=1, delay=1, lower=32, fold=1, tie_own=0, rs_tie=2, tie_k2=1, tie_act=0)


def ring_device(place, count):
    if not OPT["fold"]:
        return place
    return jnp.where(2 * place < count, 2 * place, 2 * (count - place) - 1)


def ring_place(device, count):
    if not OPT["fold"]:
        return device
    return jnp.where(device % 2 == 0, device // 2, count - (device + 1) // 2)


def shifted(block, axis, distance):
    count = lax.axis_size(axis)
    ring = list(range(count))
    if axis == "col" and OPT["fold"]:
        ring = ring[::2] + ring[1::2][::-1]
    return lax.ppermute(block, axis, [(ring[i], ring[(i + distance) % count]) for i in range(count)])


def one_hot(shape, rule):
    rows = lax.broadcasted_iota(jnp.int32, shape, 0)
    cols = lax.broadcasted_iota(jnp.int32, shape, 1)
    return jnp.where(rule(rows, cols), 1.0, 0.0).astype(BF16)


def dot(left, right):
    return jnp.dot(left, right, preferred_element_type=F32)


def fill_taps(blocks, chans, span_z, taps_ref, first_row):
    half_z = span_z // 2
    size = chans * ROWS
    swap = one_hot((size, size), lambda r, c: c == (r % chans) * ROWS + r // chans)
    split = one_hot(
        (span_z, 3 * half_z),
        lambda z, m: z == (2 * (m % half_z) + m // half_z + span_z - 1) % span_z,
    )
    pair = 2 * chans
    beside = jnp.concatenate([values() for values, _, _, _ in blocks], axis=1)
    swapped = dot(swap, beside).astype(BF16)
    below = [swapped[:, i * span_z : (i + 1) * span_z] for i in range(len(blocks))]
    tapped = dot(jnp.concatenate(below, axis=0), split).astype(BF16)
    for index, (_, first, count, place) in enumerate(blocks):
        for j in range(count):
            for tap in range(3):
                source = index * size + (first + j) * pair
                row = first_row + tap * pair
                lane = (place + j) * half_z
                taps_ref[row : row + pair, lane : lane + half_z] = tapped[
                    source : source + pair, tap * half_z : (tap + 1) * half_z
                ]


def rows_of(ref, index, block):
    def values():
        rows = ref[(slice(None), *index, slice(block * ROWS, (block + 1) * ROWS))]
        return rows.reshape(rows.shape[0] * ROWS, rows.shape[-1])

    return values


def tap_sums(weights, taps_ref, lane, width, half_z):
    before = taps_ref[:, lane : lane + width]
    here = taps_ref[:, lane + half_z : lane + half_z + width]
    return dot(weights, jnp.concatenate([before, here], axis=0))


def local_kernel(field_ref, weight_ref, acc_ref, taps_ref):
    chans, planes, span_y, span_z = field_ref.shape
    half_z = span_z // 2
    count = span_y // ROWS
    for plane in range(planes):
        blocks = [(rows_of(field_ref, (plane,), b), 0, 8, 1 + 8 * b) for b in range(count)]
        fill_taps(blocks, chans, span_z, taps_ref, plane * 6 * chans)
    taps_ref[:, :half_z] = taps_ref[:, count * 8 * half_z :]
    weights = weight_ref[...]
    width = 8 * half_z
    for step in range(count):
        lane = step * width
        acc_ref[:, lane : lane + width] = tap_sums(weights, taps_ref, lane, width, half_z)


def halo_kernel(part, *refs):
    halo_refs, (weight_ref, acc_ref), part_refs, taps_ref = (
        refs[: part + 1],
        refs[part + 1 : part + 3],
        refs[part + 3 : -1],
        refs[-1],
    )
    chans, _, span_z = halo_refs[0].shape
    half_z = span_z // 2
    lower = halo_refs[0].shape[1] // ROWS - 1
    if part == 0:
        blocks = [(rows_of(halo_refs[0], (), 0), 7, 1, 0)]
        blocks += [(rows_of(halo_refs[0], (), 1 + b), 0, 8, 1 + 8 * b) for b in range(lower)]
    else:
        upper = halo_refs[1].shape[1] // ROWS
        blocks = [(rows_of(halo_refs[0], (), lower), 7, 1, 0)]
        blocks += [(rows_of(halo_refs[1], (), b), 0, 8, 1 + 8 * b) for b in range(upper)]
        blocks += [(rows_of(halo_refs[0], (), 0), 0, 8, 1 + 8 * upper)]
    fill_taps(blocks, chans, span_z, taps_ref, 0)
    weights = weight_ref[...]
    count, rows, _ = part_refs[0].shape
    width = 8 * half_z
    base = part * (acc_ref.shape[1] - count * half_z)
    for step in range(count // 8):
        lane = step * width
        sums = acc_ref[:, base + lane : base + lane + width]
        sums = (sums + tap_sums(weights, taps_ref, lane, width, half_z)).astype(BF16)
        for j in range(8):
            for peer, ref in enumerate(part_refs):
                ref[step * 8 + j] = sums[
                    peer * rows : (peer + 1) * rows, j * half_z : (j + 1) * half_z
                ]


def add_kernel(one_ref, two_ref, sum_ref):
    sum_ref[...] = (one_ref[...].astype(F32) + two_ref[...].astype(F32)).astype(BF16)


def act_kernel(*refs):
    *part_refs, bias_ref, cot_ref, out_ref, masked_ref = refs
    pre = bias_ref[...] + functools.reduce(
        lambda a, b: a + b, [ref[...].astype(F32) for ref in part_refs]
    )
    small = jnp.exp(-jnp.abs(pre))
    soft = jnp.maximum(pre, 0.0) + jnp.log(1.0 + small)
    out_ref[...] = (0.3 * pre + 0.7 * soft).astype(BF16)
    gate = jnp.where(pre >= 0.0, 1.0, small) / (1.0 + small)
    masked_ref[...] = (cot_ref[...].astype(F32) * (0.3 + 0.7 * gate)).astype(BF16)


def grad_blocks(held_ref, weights, blocks, chans, span_z, store):
    half_z = span_z // 2
    size = chans * ROWS
    swap = one_hot((size, size), lambda r, c: c == (r % ROWS) * chans + r // ROWS)
    weave = one_hot((span_z, span_z), lambda m, z: z == 2 * (m % half_z) + m // half_z)
    pair = 2 * chans
    width = blocks * 8 * half_z
    here, after = held_ref[:, :width], held_ref[:, half_z : half_z + width]
    sums = dot(weights, jnp.concatenate([here, after], axis=0))
    beside = []
    for step in range(blocks):
        for parity_x in range(2):
            base = parity_x * 3 * pair
            rows = []
            for j in range(step * 8, step * 8 + 8):
                tile = sums[base : base + 3 * pair, j * half_z : (j + 1) * half_z]
                even = tile[:pair]
                odd = tile[pair : 2 * pair] + pltpu.roll(tile[2 * pair :], half_z - 1, 1)
                rows.append(jnp.concatenate([even.astype(BF16), odd.astype(BF16)], axis=1))
            beside.append(jnp.concatenate(rows, axis=0))
    swapped = dot(swap, jnp.concatenate(beside, axis=1)).astype(BF16)
    below = [swapped[:, i * span_z : (i + 1) * span_z] for i in range(2 * blocks)]
    woven = dot(jnp.concatenate(below, axis=0), weave).astype(BF16)
    for step in range(blocks):
        for parity_x in range(2):
            for chan in range(chans):
                first = (step * 2 + parity_x) * size + chan * ROWS
                store(chan, parity_x, step, woven[first : first + ROWS])


def lower_grad_kernel(pieces, *refs):
    *piece_refs, weight_ref, grad_ref, held_ref = refs
    chans, _, span_y, span_z = grad_ref.shape
    half_z = span_z // 2
    for index, ((number, first), _) in enumerate(pieces):
        row = index * ROWS
        for j in range(span_y // 2 + 1):
            held_ref[row : row + ROWS, j * half_z : (j + 1) * half_z] = piece_refs[number][first + j]

    def store(chan, parity_x, step, values):
        grad_ref[chan, parity_x, step * ROWS : (step + 1) * ROWS, :] = values

    grad_blocks(held_ref, weight_ref[...], span_y // ROWS, chans, span_z, store)


def upper_grad_kernel(pieces, counts, *refs):
    *piece_refs, weight_ref, lower_ref, grad_ref, held_ref = refs
    chans, _, span_y, span_z = grad_ref.shape
    half_z = span_z // 2
    done = lower_ref.shape[2]
    grad_ref[:, :, :done, :] = lower_ref[...]
    for index, ((low, low_first), (high, high_first)) in enumerate(pieces):
        row = index * ROWS
        tiles = [(low, low_first + j) for j in range(done // 2, counts[0])]
        tiles += [(high, high_first + j) for j in range(counts[1])] + [(low, low_first)]
        for place, (number, j) in enumerate(tiles):
            held_ref[row : row + ROWS, place * half_z : (place + 1) * half_z] = piece_refs[number][j]

    def store(chan, parity_x, step, values):
        first = done + step * ROWS
        grad_ref[chan, parity_x, first : first + ROWS, :] = values

    grad_blocks(held_ref, weight_ref[...], (span_y - done) // ROWS, chans, span_z, store)


def weights_kernel(peers, me_ref, own_ref, local_ref, halo_ref, back_ref):
    _, chans, total = own_ref.shape
    rows = total // peers
    place = ring_place(me_ref[0], peers)

    def tile(tap_x, tap_y, tap_z):
        return own_ref[(tap_x * 3 + tap_y) * 3 + tap_z].astype(F32)

    none = jnp.zeros((chans, total), F32)

    def ahead(r, c):
        return c == ring_device((place + r // rows) % peers, peers) * rows + r % rows

    pick = one_hot((total, total), ahead)
    for ref, taps_x in ((local_ref, (1, 2)), (halo_ref, (0,))):
        tiles = [
            none if tap_y < 0 else tile(tap_x, tap_y, tap_z)
            for taps_y in ((-1, 0), (1, 2))
            for tap_x in taps_x
            for tap_z in range(3)
            for tap_y in taps_y
        ]
        stack = jnp.concatenate(tiles, axis=0).astype(BF16)
        ref[...] = lax.dot_general(
            pick, stack, (((1,), (1,)), ((), ())), preferred_element_type=F32
        ).astype(BF16)

    back = jnp.zeros(back_ref.shape, F32)
    by_offset = ((1, 2), (-1, 0))
    for offset in range(2):
        for plane in range(2):
            tiles = [
                none if min(tap_x, tap_y) < 0 else tile(tap_x, tap_y, tap_z)
                for tap_x in by_offset[plane]
                for tap_z in (1, 2, 0)
                for tap_y in by_offset[offset]
            ]
            stack = jnp.concatenate(tiles, axis=0).astype(BF16)
            first = (offset * 2 + plane) * total

            def behind(r, c, first=first):
                c = c - first
                device = ring_device((place + peers - c // rows) % peers, peers)
                return (r == device * rows + c % rows) & (c >= 0) & (c < total)

            back = back + dot(stack, one_hot((total, 4 * total), behind))
    back_ref[...] = back.astype(BF16)


def call(kernel, name, out_shape, args, scratch=(), flops=0, bytes_accessed=1 << 20, transcendentals=0):
    return pl.pallas_call(
        kernel,
        out_shape=out_shape,
        scratch_shapes=list(scratch),
        compiler_params=PARAMS,
        cost_estimate=pl.CostEstimate(
            flops=flops, bytes_accessed=bytes_accessed, transcendentals=transcendentals
        ),
        name=name,
    )(*args)


def on_device(field, kernel, bias, cotangent):
    peers = lax.axis_size("col")
    me = lax.axis_index("col")
    quarter = peers // 4
    cin, planes, span_y, span_z = field.shape
    cout = bias.shape[0]
    half_y, half_z = span_y // 2, span_z // 2
    counts = (OPT["lower"], half_y - OPT["lower"])
    starts = (0, counts[0])
    mid = 2 * counts[0]
    last = span_y - ROWS
    plane = lax.optimization_barrier(field[:, planes - 1])
    halos = [jnp.concatenate([plane[:, last:], plane[:, :mid]], axis=1), plane[:, mid:last]]
    halos = [shifted(halo, "gx", 1) for halo in halos]

    chans = -(-cin // 8) * 8
    rows = -(-cout // ROWS) * ROWS
    total = peers * rows
    fill_c = (0, chans - cin)
    fill_o = (0, rows - cout)
    own = lax.dynamic_slice_in_dim(jnp.transpose(kernel, (2, 3, 4, 1, 0)), me * cin, cin, 3)
    own = own.reshape(27, cin, peers, cout)
    own = jnp.pad(own, ((0, 0), fill_c, (0, 0), fill_o)).reshape(27, chans, total)
    field_p = jnp.pad(field, (fill_c, (0, 0), (0, 0), (0, 0)))

    points = half_y * half_z
    vmem = pl.BlockSpec(memory_space=pltpu.VMEM)
    weights_local, weights_halo, weights_back = pl.pallas_call(
        functools.partial(weights_kernel, peers),
        out_shape=[
            jax.ShapeDtypeStruct((total, 24 * chans), BF16),
            jax.ShapeDtypeStruct((total, 12 * chans), BF16),
            jax.ShapeDtypeStruct((12 * chans, 4 * total), BF16),
        ],
        in_specs=[pl.BlockSpec(memory_space=pltpu.SMEM), vmem],
        out_specs=[vmem] * 3,
        compiler_params=PARAMS,
        cost_estimate=pl.CostEstimate(flops=1 << 27, bytes_accessed=1 << 19, transcendentals=0),
        name="weights",
    )(me.astype(jnp.int32).reshape(1), own)
    acc = call(
        local_kernel,
        "local_planes",
        jax.ShapeDtypeStruct((total, points), F32),
        (field_p, weights_local),
        [
            pltpu.VMEM((planes * 6 * chans, (1 + half_y) * half_z), BF16),
        ],
        flops=2 * total * 24 * chans * points,
        bytes_accessed=1 << 22,
    )
    halos = [jnp.pad(halo, (fill_c, (0, 0), (0, 0))) for halo in halos]
    shapes = [jax.ShapeDtypeStruct((count, rows, half_z), BF16) for count in counts]
    parts = []
    for part in range(2):
        if part and OPT["tie_k2"]:
            weights_halo, parts[0] = lax.optimization_barrier((weights_halo, parts[0]))
        parts.append(
            call(
                functools.partial(halo_kernel, part),
                "halo_plane",
                [shapes[part]] * peers,
                (*halos[: part + 1], weights_halo, acc),
                [pltpu.VMEM((6 * chans, (1 + counts[part]) * half_z), BF16)],
                flops=total * 12 * chans * points,
                bytes_accessed=1 << 21,
            )
        )

    far = 2 * quarter
    steps = (quarter, peers - quarter)
    arrived = [[parts[h][0]] for h in range(2)]
    relayed = [shifted(parts[h][far], "col", steps[h]) if OPT["rs_relay"][h] else None for h in range(2)]
    for h in range(2):
        for r in range(1, peers):
            if not OPT["rs_relay"][h] or r not in (steps[h], far):
                sent = parts[h][r]
                if h and OPT["rs_tie"] >= 2:
                    sent, relayed[0] = lax.optimization_barrier((sent, relayed[0]))
                arrived[h].append(shifted(sent, "col", r))
    for h in range(2):
        if OPT["rs_tie"] == 1 or (OPT["rs_tie"] >= 3 and h == 0):
            relayed[h], arrived[h] = lax.optimization_barrier((relayed[h], arrived[h]))
        if OPT["rs_relay"][h]:
            joined = call(add_kernel, "add", shapes[h], (relayed[h], parts[h][steps[h]]))
            arrived[h].append(shifted(joined, "col", steps[h]))

    bias_p = jnp.broadcast_to(jnp.pad(bias, fill_o)[None, :, None], (1, rows, half_z))
    cot = jnp.pad(jnp.transpose(cotangent[:, 0], (1, 0, 2)), ((0, 0), fill_o, (0, 0)))
    acts = []
    for h in range(2):
        if h and OPT['tie_act']:
            bias_p, acts[0] = lax.optimization_barrier((bias_p, acts[0]))
        acts.append(
            call(
                act_kernel,
                "activation",
                (shapes[h], shapes[h]),
                (*arrived[h], bias_p, cot[starts[h] : starts[h] + counts[h]]),
                transcendentals=3 * counts[h] * rows * half_z,
            )
        )
    out = jnp.concatenate([out for out, _ in acts], axis=0)
    out_act = jnp.transpose(out[:, :cout], (1, 0, 2))[:, None]

    masked = [masked for _, masked in acts]
    gathered = [{0: masked[h]} for h in range(2)]
    for h in range(2):
        for r in range(1, peers):
            if r != far or not OPT["ag_relay"][h]:
                gathered[h][r] = shifted(masked[h], "col", r)
    above = [{}, {}]
    arrays = []

    def spec(value, *at):
        arrays.append(value)
        return len(arrays) - 1

    if OPT["gx_merge"]:
        whole = shifted(jnp.concatenate(masked, axis=0), "gx", -1)
        number = spec(whole)
        for h in range(2):
            above[h][0] = (number, starts[h])
    else:
        for h in range(2):
            above[h][0] = (spec(shifted(masked[h], "gx", -1)), 0)
    for h in range(2):
        if OPT["ag_tie"] == 1 or (OPT["ag_tie"] and h == 0):
            gathered[h] = lax.optimization_barrier(gathered[h])
        if h == 1 and OPT["tie_own"]:
            gathered[1][steps[1]], whole = lax.optimization_barrier((gathered[1][steps[1]], arrays[0]))
            arrays[0] = whole
    for h in range(2):
        near = [r for r in range(1, peers) if r != far]
        if OPT["gx_merge"]:
            number = spec(shifted(jnp.concatenate([gathered[h][r] for r in near], axis=0), "gx", -1))
            for i, r in enumerate(near):
                above[h][r] = (number, i * counts[h])
        else:
            for r in near:
                above[h][r] = (spec(shifted(gathered[h][r], "gx", -1)), 0)
    for h in range(2):
        if OPT["ag_relay"][h]:
            gathered[h][far] = shifted(gathered[h][steps[h]], "col", steps[h])
        if OPT["ag_tie"] == 3 and h == 0:
            both = (gathered[0][far], gathered[1][steps[0]])
            gathered[0][far], gathered[1][steps[0]] = lax.optimization_barrier(both)
        if OPT["ag_tie"] == 4 and h == 0:
            both = (gathered[0][far], gathered[1][steps[0]], gathered[1][steps[1]])
            gathered[0][far], gathered[1][steps[0]], gathered[1][steps[1]] = lax.optimization_barrier(both)
        above[h][far] = (spec(shifted(gathered[h][far], "gx", -1)), 0)
    mine = [{r: (spec(gathered[h][r]), 0) for r in range(peers)} for h in range(2)]
    order = [[places[h][r] for h in range(2)] for places in (mine, above) for r in range(peers)]

    def grad_call(kernel, name, shape, used, extra, blocks):
        used = sorted(used)
        renamed = [[(used.index(n) if n in used else -1, at) for n, at in both] for both in order]
        return call(
            functools.partial(kernel, renamed),
            name,
            shape,
            (*[arrays[n] for n in used], weights_back, *extra),
            [
                pltpu.VMEM((2 * total, (1 + 8 * blocks) * half_z), BF16),
            ],
            flops=8 * total * 12 * chans * 8 * blocks * half_z,
        )

    done = mid - ROWS
    lower = grad_call(
        lower_grad_kernel,
        "lower_grad",
        jax.ShapeDtypeStruct((chans, planes, done, span_z), BF16),
        {both[0][0] for both in order},
        (),
        done // ROWS,
    )
    in_grad = grad_call(
        lambda pieces, *refs: upper_grad_kernel(pieces, counts, *refs),
        "upper_grad",
        jax.ShapeDtypeStruct((chans, planes, span_y, span_z), BF16),
        {n for both in order for n, _ in both},
        (lower,),
        (span_y - done) // ROWS,
    )
    return out_act, in_grad[:cin]


def solution(mesh):
    in_specs = (P("col", "gx", None, None), P(), P("col"), P("col", "gx", None, None))
    out_specs = (P("col", "gx", None, None), P("col", "gx", None, None))
    return jax.shard_map(
        on_device, mesh=mesh, in_specs=in_specs, out_specs=out_specs, check_vma=False
    )
```

```python
import functools

import jax
import jax.numpy as jnp
from jax import lax
from jax.experimental import pallas as pl
from jax.experimental.pallas import tpu as pltpu
from jax.sharding import PartitionSpec as P

F32 = jnp.float32
BF16 = jnp.bfloat16
LANES = 128
ROWS = 16
PARAMS = pltpu.CompilerParams(vmem_limit_bytes=24 * 1024 * 1024)


def ring_device(place, count):
    return jnp.where(2 * place < count, 2 * place, 2 * (count - place) - 1)


def ring_place(device, count):
    return jnp.where(device % 2 == 0, device // 2, count - (device + 1) // 2)


def shifted(block, axis, distance):
    count = lax.axis_size(axis)
    ring = list(range(count))
    if axis == "col":
        ring = ring[::2] + ring[1::2][::-1]
    return lax.ppermute(block, axis, [(ring[i], ring[(i + distance) % count]) for i in range(count)])


def one_hot(shape, rule):
    rows = lax.broadcasted_iota(jnp.int32, shape, 0)
    cols = lax.broadcasted_iota(jnp.int32, shape, 1)
    return jnp.where(rule(rows, cols), 1.0, 0.0).astype(BF16)


def dot(left, right):
    return jnp.dot(left, right, preferred_element_type=F32)


def fill_taps(blocks, chans, span_z, taps_ref, first_row):
    half_z = span_z // 2
    size = chans * ROWS
    swap = one_hot((size, size), lambda r, c: c == (r % chans) * ROWS + r // chans)
    split = one_hot(
        (span_z, 3 * half_z),
        lambda z, m: z == (2 * (m % half_z) + m // half_z + span_z - 1) % span_z,
    )
    pair = 2 * chans
    beside = jnp.concatenate([values() for values, _, _, _ in blocks], axis=1)
    swapped = dot(swap, beside).astype(BF16)
    below = [swapped[:, i * span_z : (i + 1) * span_z] for i in range(len(blocks))]
    tapped = dot(jnp.concatenate(below, axis=0), split).astype(BF16)
    for index, (_, first, count, place) in enumerate(blocks):
        for j in range(count):
            for tap in range(3):
                source = index * size + (first + j) * pair
                row = first_row + tap * pair
                lane = (place + j) * half_z
                taps_ref[row : row + pair, lane : lane + half_z] = tapped[
                    source : source + pair, tap * half_z : (tap + 1) * half_z
                ]


def rows_of(ref, index, block):
    def values():
        rows = ref[(slice(None), *index, slice(block * ROWS, (block + 1) * ROWS))]
        return rows.reshape(rows.shape[0] * ROWS, rows.shape[-1])

    return values


def tap_sums(weights, taps_ref, lane, width, half_z):
    before = taps_ref[:, lane : lane + width]
    here = taps_ref[:, lane + half_z : lane + half_z + width]
    return dot(weights, jnp.concatenate([before, here], axis=0))


def local_kernel(field_ref, weight_ref, acc_ref, taps_ref):
    chans, planes, span_y, span_z = field_ref.shape
    half_z = span_z // 2
    count = span_y // ROWS
    for plane in range(planes):
        blocks = [(rows_of(field_ref, (plane,), b), 0, 8, 1 + 8 * b) for b in range(count)]
        fill_taps(blocks, chans, span_z, taps_ref, plane * 6 * chans)
    taps_ref[:, :half_z] = taps_ref[:, count * 8 * half_z :]
    weights = weight_ref[...]
    width = 8 * half_z
    for step in range(count):
        lane = step * width
        acc_ref[:, lane : lane + width] = tap_sums(weights, taps_ref, lane, width, half_z)


def halo_kernel(part, *refs):
    halo_refs, (weight_ref, acc_ref), part_refs, taps_ref = (
        refs[: part + 1],
        refs[part + 1 : part + 3],
        refs[part + 3 : -1],
        refs[-1],
    )
    chans, _, span_z = halo_refs[0].shape
    half_z = span_z // 2
    lower = halo_refs[0].shape[1] // ROWS - 1
    if part == 0:
        blocks = [(rows_of(halo_refs[0], (), 0), 7, 1, 0)]
        blocks += [(rows_of(halo_refs[0], (), 1 + b), 0, 8, 1 + 8 * b) for b in range(lower)]
    else:
        upper = halo_refs[1].shape[1] // ROWS
        blocks = [(rows_of(halo_refs[0], (), lower), 7, 1, 0)]
        blocks += [(rows_of(halo_refs[1], (), b), 0, 8, 1 + 8 * b) for b in range(upper)]
        blocks += [(rows_of(halo_refs[0], (), 0), 0, 8, 1 + 8 * upper)]
    fill_taps(blocks, chans, span_z, taps_ref, 0)
    weights = weight_ref[...]
    count, rows, _ = part_refs[0].shape
    width = 8 * half_z
    base = part * (acc_ref.shape[1] - count * half_z)
    for step in range(count // 8):
        lane = step * width
        sums = acc_ref[:, base + lane : base + lane + width]
        sums = (sums + tap_sums(weights, taps_ref, lane, width, half_z)).astype(BF16)
        for j in range(8):
            for peer, ref in enumerate(part_refs):
                ref[step * 8 + j] = sums[
                    peer * rows : (peer + 1) * rows, j * half_z : (j + 1) * half_z
                ]


def add_kernel(one_ref, two_ref, sum_ref):
    sum_ref[...] = (one_ref[...].astype(F32) + two_ref[...].astype(F32)).astype(BF16)


def act_kernel(*refs):
    *part_refs, bias_ref, cot_ref, out_ref, masked_ref = refs
    pre = bias_ref[...] + functools.reduce(
        lambda a, b: a + b, [ref[...].astype(F32) for ref in part_refs]
    )
    small = jnp.exp(-jnp.abs(pre))
    soft = jnp.maximum(pre, 0.0) + jnp.log(1.0 + small)
    out_ref[...] = (0.3 * pre + 0.7 * soft).astype(BF16)
    gate = jnp.where(pre >= 0.0, 1.0, small) / (1.0 + small)
    masked_ref[...] = (cot_ref[...].astype(F32) * (0.3 + 0.7 * gate)).astype(BF16)


def grad_blocks(held_ref, weights, blocks, chans, span_z, store):
    half_z = span_z // 2
    size = chans * ROWS
    swap = one_hot((size, size), lambda r, c: c == (r % ROWS) * chans + r // ROWS)
    weave = one_hot((span_z, span_z), lambda m, z: z == 2 * (m % half_z) + m // half_z)
    pair = 2 * chans
    width = blocks * 8 * half_z
    here, after = held_ref[:, :width], held_ref[:, half_z : half_z + width]
    sums = dot(weights, jnp.concatenate([here, after], axis=0))
    beside = []
    for step in range(blocks):
        for parity_x in range(2):
            base = parity_x * 3 * pair
            rows = []
            for j in range(step * 8, step * 8 + 8):
                tile = sums[base : base + 3 * pair, j * half_z : (j + 1) * half_z]
                even = tile[:pair]
                odd = tile[pair : 2 * pair] + pltpu.roll(tile[2 * pair :], half_z - 1, 1)
                rows.append(jnp.concatenate([even.astype(BF16), odd.astype(BF16)], axis=1))
            beside.append(jnp.concatenate(rows, axis=0))
    swapped = dot(swap, jnp.concatenate(beside, axis=1)).astype(BF16)
    below = [swapped[:, i * span_z : (i + 1) * span_z] for i in range(2 * blocks)]
    woven = dot(jnp.concatenate(below, axis=0), weave).astype(BF16)
    for step in range(blocks):
        for parity_x in range(2):
            for chan in range(chans):
                first = (step * 2 + parity_x) * size + chan * ROWS
                store(chan, parity_x, step, woven[first : first + ROWS])


def lower_grad_kernel(pieces, *refs):
    *piece_refs, weight_ref, grad_ref, held_ref = refs
    chans, _, span_y, span_z = grad_ref.shape
    half_z = span_z // 2
    for index, ((number, first), _) in enumerate(pieces):
        row = index * ROWS
        for j in range(span_y // 2 + 1):
            held_ref[row : row + ROWS, j * half_z : (j + 1) * half_z] = piece_refs[number][first + j]

    def store(chan, parity_x, step, values):
        grad_ref[chan, parity_x, step * ROWS : (step + 1) * ROWS, :] = values

    grad_blocks(held_ref, weight_ref[...], span_y // ROWS, chans, span_z, store)


def upper_grad_kernel(pieces, counts, *refs):
    *piece_refs, weight_ref, lower_ref, grad_ref, held_ref = refs
    chans, _, span_y, span_z = grad_ref.shape
    half_z = span_z // 2
    done = lower_ref.shape[2]
    grad_ref[:, :, :done, :] = lower_ref[...]
    for index, ((low, low_first), (high, high_first)) in enumerate(pieces):
        row = index * ROWS
        tiles = [(low, low_first + j) for j in range(done // 2, counts[0])]
        tiles += [(high, high_first + j) for j in range(counts[1])] + [(low, low_first)]
        for place, (number, j) in enumerate(tiles):
            held_ref[row : row + ROWS, place * half_z : (place + 1) * half_z] = piece_refs[number][j]

    def store(chan, parity_x, step, values):
        first = done + step * ROWS
        grad_ref[chan, parity_x, first : first + ROWS, :] = values

    grad_blocks(held_ref, weight_ref[...], (span_y - done) // ROWS, chans, span_z, store)


def weights_kernel(peers, me_ref, own_ref, local_ref, halo_ref, back_ref):
    _, chans, total = own_ref.shape
    rows = total // peers
    place = ring_place(me_ref[0], peers)

    def tile(tap_x, tap_y, tap_z):
        return own_ref[(tap_x * 3 + tap_y) * 3 + tap_z].astype(F32)

    none = jnp.zeros((chans, total), F32)

    def ahead(r, c):
        return c == ring_device((place + r // rows) % peers, peers) * rows + r % rows

    pick = one_hot((total, total), ahead)
    for ref, taps_x in ((local_ref, (1, 2)), (halo_ref, (0,))):
        tiles = [
            none if tap_y < 0 else tile(tap_x, tap_y, tap_z)
            for taps_y in ((-1, 0), (1, 2))
            for tap_x in taps_x
            for tap_z in range(3)
            for tap_y in taps_y
        ]
        stack = jnp.concatenate(tiles, axis=0).astype(BF16)
        ref[...] = lax.dot_general(
            pick, stack, (((1,), (1,)), ((), ())), preferred_element_type=F32
        ).astype(BF16)

    back = jnp.zeros(back_ref.shape, F32)
    by_offset = ((1, 2), (-1, 0))
    for offset in range(2):
        for plane in range(2):
            tiles = [
                none if min(tap_x, tap_y) < 0 else tile(tap_x, tap_y, tap_z)
                for tap_x in by_offset[plane]
                for tap_z in (1, 2, 0)
                for tap_y in by_offset[offset]
            ]
            stack = jnp.concatenate(tiles, axis=0).astype(BF16)
            first = (offset * 2 + plane) * total

            def behind(r, c, first=first):
                c = c - first
                device = ring_device((place + peers - c // rows) % peers, peers)
                return (r == device * rows + c % rows) & (c >= 0) & (c < total)

            back = back + dot(stack, one_hot((total, 4 * total), behind))
    back_ref[...] = back.astype(BF16)


def call(kernel, name, out_shape, args, scratch=(), flops=0, bytes_accessed=1 << 20, transcendentals=0):
    return pl.pallas_call(
        kernel,
        out_shape=out_shape,
        scratch_shapes=list(scratch),
        compiler_params=PARAMS,
        cost_estimate=pl.CostEstimate(
            flops=flops, bytes_accessed=bytes_accessed, transcendentals=transcendentals
        ),
        name=name,
    )(*args)


def on_device(field, kernel, bias, cotangent):
    peers = lax.axis_size("col")
    me = lax.axis_index("col")
    quarter = peers // 4
    cin, planes, span_y, span_z = field.shape
    cout = bias.shape[0]
    half_y, half_z = span_y // 2, span_z // 2
    counts = (half_y // 2, half_y - half_y // 2)
    starts = (0, counts[0])
    mid = 2 * counts[0]
    last = span_y - ROWS
    plane = lax.optimization_barrier(field[:, planes - 1])
    halos = [jnp.concatenate([plane[:, last:], plane[:, :mid]], axis=1), plane[:, mid:last]]
    halos = [shifted(halo, "gx", 1) for halo in halos]

    chans = -(-cin // 8) * 8
    rows = -(-cout // ROWS) * ROWS
    total = peers * rows
    fill_c = (0, chans - cin)
    fill_o = (0, rows - cout)
    own = lax.dynamic_slice_in_dim(jnp.transpose(kernel, (2, 3, 4, 1, 0)), me * cin, cin, 3)
    own = own.reshape(27, cin, peers, cout)
    own = jnp.pad(own, ((0, 0), fill_c, (0, 0), fill_o)).reshape(27, chans, total)
    field_p = jnp.pad(field, (fill_c, (0, 0), (0, 0), (0, 0)))

    points = half_y * half_z
    vmem = pl.BlockSpec(memory_space=pltpu.VMEM)
    weights_local, weights_halo, weights_back = pl.pallas_call(
        functools.partial(weights_kernel, peers),
        out_shape=[
            jax.ShapeDtypeStruct((total, 24 * chans), BF16),
            jax.ShapeDtypeStruct((total, 12 * chans), BF16),
            jax.ShapeDtypeStruct((12 * chans, 4 * total), BF16),
        ],
        in_specs=[pl.BlockSpec(memory_space=pltpu.SMEM), vmem],
        out_specs=[vmem] * 3,
        compiler_params=PARAMS,
        cost_estimate=pl.CostEstimate(flops=1 << 27, bytes_accessed=1 << 19, transcendentals=0),
        name="weights",
    )(me.astype(jnp.int32).reshape(1), own)
    acc = call(
        local_kernel,
        "local_planes",
        jax.ShapeDtypeStruct((total, points), F32),
        (field_p, weights_local),
        [
            pltpu.VMEM((planes * 6 * chans, (1 + half_y) * half_z), BF16),
        ],
        flops=2 * total * 24 * chans * points,
        bytes_accessed=1 << 22,
    )
    halos = [jnp.pad(halo, (fill_c, (0, 0), (0, 0))) for halo in halos]
    shapes = [jax.ShapeDtypeStruct((count, rows, half_z), BF16) for count in counts]
    parts = []
    for part in range(2):
        if part:
            weights_halo, parts[0] = lax.optimization_barrier((weights_halo, parts[0]))
        parts.append(
            call(
                functools.partial(halo_kernel, part),
                "halo_plane",
                [shapes[part]] * peers,
                (*halos[: part + 1], weights_halo, acc),
                [pltpu.VMEM((6 * chans, (1 + counts[part]) * half_z), BF16)],
                flops=total * 12 * chans * points,
                bytes_accessed=1 << 21,
            )
        )

    far = 2 * quarter
    steps = (quarter, peers - quarter)
    arrived = [[parts[h][0]] for h in range(2)]
    relayed = [shifted(parts[h][far], "col", steps[h]) for h in range(2)]
    for h in range(2):
        for r in range(1, peers):
            if r not in (steps[h], far):
                sent = parts[h][r]
                if h:
                    sent, relayed[0] = lax.optimization_barrier((sent, relayed[0]))
                arrived[h].append(shifted(sent, "col", r))
    for h in range(2):
        if h:
            relayed[1], arrived[0][-1] = lax.optimization_barrier((relayed[1], arrived[0][-1]))
        joined = call(add_kernel, "add", shapes[h], (relayed[h], parts[h][steps[h]]))
        arrived[h].append(shifted(joined, "col", steps[h]))

    bias_p = jnp.broadcast_to(jnp.pad(bias, fill_o)[None, :, None], (1, rows, half_z))
    cot = jnp.pad(jnp.transpose(cotangent[:, 0], (1, 0, 2)), ((0, 0), fill_o, (0, 0)))
    acts = [
        call(
            act_kernel,
            "activation",
            (shapes[h], shapes[h]),
            (*arrived[h], bias_p, cot[starts[h] : starts[h] + counts[h]]),
            transcendentals=3 * counts[h] * rows * half_z,
        )
        for h in range(2)
    ]
    out = jnp.concatenate([out for out, _ in acts], axis=0)
    out_act = jnp.transpose(out[:, :cout], (1, 0, 2))[:, None]

    masked = [masked for _, masked in acts]
    near = [r for r in range(1, peers) if r != far]
    gathered = [{0: masked[h], **{r: shifted(masked[h], "col", r) for r in near}} for h in range(2)]
    above = [{}, {}]
    arrays = []

    def place_of(value):
        arrays.append(value)
        return len(arrays) - 1

    whole = place_of(shifted(jnp.concatenate(masked, axis=0), "gx", -1))
    for h in range(2):
        above[h][0] = (whole, starts[h])
    gathered[0] = lax.optimization_barrier(gathered[0])
    for h in range(2):
        joined = jnp.concatenate([gathered[h][r] for r in near], axis=0)
        number = place_of(shifted(joined, "gx", -1))
        for i, r in enumerate(near):
            above[h][r] = (number, i * counts[h])
    for h in range(2):
        gathered[h][far] = shifted(gathered[h][steps[h]], "col", steps[h])
        above[h][far] = (place_of(shifted(gathered[h][far], "gx", -1)), 0)
    mine = [{r: (place_of(gathered[h][r]), 0) for r in range(peers)} for h in range(2)]
    order = [[places[h][r] for h in range(2)] for places in (mine, above) for r in range(peers)]

    def grad_call(kernel, name, shape, used, extra, blocks):
        used = sorted(used)
        renamed = [[(used.index(n) if n in used else -1, at) for n, at in both] for both in order]
        return call(
            functools.partial(kernel, renamed),
            name,
            shape,
            (*[arrays[n] for n in used], weights_back, *extra),
            [
                pltpu.VMEM((2 * total, (1 + 8 * blocks) * half_z), BF16),
            ],
            flops=8 * total * 12 * chans * 8 * blocks * half_z,
        )

    done = mid - ROWS
    lower = grad_call(
        lower_grad_kernel,
        "lower_grad",
        jax.ShapeDtypeStruct((chans, planes, done, span_z), BF16),
        {both[0][0] for both in order},
        (),
        done // ROWS,
    )
    in_grad = grad_call(
        lambda pieces, *refs: upper_grad_kernel(pieces, counts, *refs),
        "upper_grad",
        jax.ShapeDtypeStruct((chans, planes, span_y, span_z), BF16),
        {n for both in order for n, _ in both},
        (lower,),
        (span_y - done) // ROWS,
    )
    return out_act, in_grad[:cin]


def solution(mesh):
    in_specs = (P("col", "gx", None, None), P(), P("col"), P("col", "gx", None, None))
    out_specs = (P("col", "gx", None, None), P("col", "gx", None, None))
    return jax.shard_map(
        on_device, mesh=mesh, in_specs=in_specs, out_specs=out_specs, check_vma=False
    )
```

```python
import functools

import jax
import jax.numpy as jnp
from jax import lax
from jax.experimental import pallas as pl
from jax.experimental.pallas import tpu as pltpu
from jax.sharding import PartitionSpec as P

F32 = jnp.float32
BF16 = jnp.bfloat16
LANES = 128
ROWS = 16
PARAMS = pltpu.CompilerParams(vmem_limit_bytes=24 * 1024 * 1024)


def ring_device(place, count):
    return jnp.where(2 * place < count, 2 * place, 2 * (count - place) - 1)


def ring_place(device, count):
    return jnp.where(device % 2 == 0, device // 2, count - (device + 1) // 2)


def shifted(block, axis, distance):
    count = lax.axis_size(axis)
    ring = list(range(count))
    if axis == "col":
        ring = ring[::2] + ring[1::2][::-1]
    return lax.ppermute(block, axis, [(ring[i], ring[(i + distance) % count]) for i in range(count)])


def one_hot(shape, rule):
    rows = lax.broadcasted_iota(jnp.int32, shape, 0)
    cols = lax.broadcasted_iota(jnp.int32, shape, 1)
    return jnp.where(rule(rows, cols), 1.0, 0.0).astype(BF16)


def dot(left, right):
    return jnp.dot(left, right, preferred_element_type=F32)


def fill_taps(blocks, chans, span_z, taps_ref, first_row):
    half_z = span_z // 2
    size = chans * ROWS
    swap = one_hot((size, size), lambda r, c: c == (r % chans) * ROWS + r // chans)
    split = one_hot(
        (span_z, 3 * half_z),
        lambda z, m: z == (2 * (m % half_z) + m // half_z + span_z - 1) % span_z,
    )
    pair = 2 * chans
    beside = jnp.concatenate([values() for values, _, _, _ in blocks], axis=1)
    swapped = dot(swap, beside).astype(BF16)
    below = [swapped[:, i * span_z : (i + 1) * span_z] for i in range(len(blocks))]
    tapped = dot(jnp.concatenate(below, axis=0), split).astype(BF16)
    for index, (_, first, count, place) in enumerate(blocks):
        for j in range(count):
            for tap in range(3):
                source = index * size + (first + j) * pair
                row = first_row + tap * pair
                lane = (place + j) * half_z
                taps_ref[row : row + pair, lane : lane + half_z] = tapped[
                    source : source + pair, tap * half_z : (tap + 1) * half_z
                ]


def rows_of(ref, index, block):
    def values():
        rows = ref[(slice(None), *index, slice(block * ROWS, (block + 1) * ROWS))]
        return rows.reshape(rows.shape[0] * ROWS, rows.shape[-1])

    return values


def tap_sums(weights, taps_ref, lane, width, half_z):
    before = taps_ref[:, lane : lane + width]
    here = taps_ref[:, lane + half_z : lane + half_z + width]
    return dot(weights, jnp.concatenate([before, here], axis=0))


def local_kernel(field_ref, weight_ref, acc_ref, taps_ref):
    chans, planes, span_y, span_z = field_ref.shape
    half_z = span_z // 2
    count = span_y // ROWS
    for plane in range(planes):
        blocks = [(rows_of(field_ref, (plane,), b), 0, 8, 1 + 8 * b) for b in range(count)]
        fill_taps(blocks, chans, span_z, taps_ref, plane * 6 * chans)
    taps_ref[:, :half_z] = taps_ref[:, count * 8 * half_z :]
    weights = weight_ref[...]
    width = 8 * half_z
    for step in range(count):
        lane = step * width
        acc_ref[:, lane : lane + width] = tap_sums(weights, taps_ref, lane, width, half_z)


def halo_kernel(part, *refs):
    halo_refs, (weight_ref, acc_ref), part_refs, taps_ref = (
        refs[: part + 1],
        refs[part + 1 : part + 3],
        refs[part + 3 : -1],
        refs[-1],
    )
    chans, _, span_z = halo_refs[0].shape
    half_z = span_z // 2
    lower = halo_refs[0].shape[1] // ROWS - 1
    if part == 0:
        blocks = [(rows_of(halo_refs[0], (), 0), 7, 1, 0)]
        blocks += [(rows_of(halo_refs[0], (), 1 + b), 0, 8, 1 + 8 * b) for b in range(lower)]
    else:
        upper = halo_refs[1].shape[1] // ROWS
        blocks = [(rows_of(halo_refs[0], (), lower), 7, 1, 0)]
        blocks += [(rows_of(halo_refs[1], (), b), 0, 8, 1 + 8 * b) for b in range(upper)]
        blocks += [(rows_of(halo_refs[0], (), 0), 0, 8, 1 + 8 * upper)]
    fill_taps(blocks, chans, span_z, taps_ref, 0)
    weights = weight_ref[...]
    count, rows, _ = part_refs[0].shape
    width = 8 * half_z
    base = part * (acc_ref.shape[1] - count * half_z)
    for step in range(count // 8):
        lane = step * width
        sums = acc_ref[:, base + lane : base + lane + width]
        sums = (sums + tap_sums(weights, taps_ref, lane, width, half_z)).astype(BF16)
        for j in range(8):
            for peer, ref in enumerate(part_refs):
                ref[step * 8 + j] = sums[
                    peer * rows : (peer + 1) * rows, j * half_z : (j + 1) * half_z
                ]


def add_kernel(one_ref, two_ref, sum_ref):
    sum_ref[...] = (one_ref[...].astype(F32) + two_ref[...].astype(F32)).astype(BF16)


def act_kernel(*refs):
    *part_refs, bias_ref, cot_ref, out_ref, masked_ref = refs
    pre = bias_ref[...] + functools.reduce(
        lambda a, b: a + b, [ref[...].astype(F32) for ref in part_refs]
    )
    small = jnp.exp(-jnp.abs(pre))
    soft = jnp.maximum(pre, 0.0) + jnp.log(1.0 + small)
    out_ref[...] = (0.3 * pre + 0.7 * soft).astype(BF16)
    gate = jnp.where(pre >= 0.0, 1.0, small) / (1.0 + small)
    masked_ref[...] = (cot_ref[...].astype(F32) * (0.3 + 0.7 * gate)).astype(BF16)


def grad_blocks(held_ref, weights, blocks, chans, span_z, store):
    half_z = span_z // 2
    size = chans * ROWS
    swap = one_hot((size, size), lambda r, c: c == (r % ROWS) * chans + r // ROWS)
    weave = one_hot((span_z, span_z), lambda m, z: z == 2 * (m % half_z) + m // half_z)
    pair = 2 * chans
    width = blocks * 8 * half_z
    here, after = held_ref[:, :width], held_ref[:, half_z : half_z + width]
    sums = dot(weights, jnp.concatenate([here, after], axis=0))
    beside = []
    for step in range(blocks):
        for parity_x in range(2):
            base = parity_x * 3 * pair
            rows = []
            for j in range(step * 8, step * 8 + 8):
                tile = sums[base : base + 3 * pair, j * half_z : (j + 1) * half_z]
                even = tile[:pair]
                odd = tile[pair : 2 * pair] + pltpu.roll(tile[2 * pair :], half_z - 1, 1)
                rows.append(jnp.concatenate([even.astype(BF16), odd.astype(BF16)], axis=1))
            beside.append(jnp.concatenate(rows, axis=0))
    swapped = dot(swap, jnp.concatenate(beside, axis=1)).astype(BF16)
    below = [swapped[:, i * span_z : (i + 1) * span_z] for i in range(2 * blocks)]
    woven = dot(jnp.concatenate(below, axis=0), weave).astype(BF16)
    for step in range(blocks):
        for parity_x in range(2):
            for chan in range(chans):
                first = (step * 2 + parity_x) * size + chan * ROWS
                store(chan, parity_x, step, woven[first : first + ROWS])


def lower_grad_kernel(pieces, *refs):
    *piece_refs, weight_ref, grad_ref, held_ref = refs
    chans, _, span_y, span_z = grad_ref.shape
    half_z = span_z // 2
    for index, ((number, first), _) in enumerate(pieces):
        row = index * ROWS
        for j in range(span_y // 2 + 1):
            held_ref[row : row + ROWS, j * half_z : (j + 1) * half_z] = piece_refs[number][first + j]

    def store(chan, parity_x, step, values):
        grad_ref[chan, parity_x, step * ROWS : (step + 1) * ROWS, :] = values

    grad_blocks(held_ref, weight_ref[...], span_y // ROWS, chans, span_z, store)


def upper_grad_kernel(pieces, counts, *refs):
    *piece_refs, weight_ref, lower_ref, grad_ref, held_ref = refs
    chans, _, span_y, span_z = grad_ref.shape
    half_z = span_z // 2
    done = lower_ref.shape[2]
    grad_ref[:, :, :done, :] = lower_ref[...]
    for index, ((low, low_first), (high, high_first)) in enumerate(pieces):
        row = index * ROWS
        tiles = [(low, low_first + j) for j in range(done // 2, counts[0])]
        tiles += [(high, high_first + j) for j in range(counts[1])] + [(low, low_first)]
        for place, (number, j) in enumerate(tiles):
            held_ref[row : row + ROWS, place * half_z : (place + 1) * half_z] = piece_refs[number][j]

    def store(chan, parity_x, step, values):
        first = done + step * ROWS
        grad_ref[chan, parity_x, first : first + ROWS, :] = values

    grad_blocks(held_ref, weight_ref[...], (span_y - done) // ROWS, chans, span_z, store)


def weights_kernel(peers, me_ref, own_ref, local_ref, halo_ref, back_ref):
    _, chans, total = own_ref.shape
    rows = total // peers
    place = ring_place(me_ref[0], peers)

    def tile(tap_x, tap_y, tap_z):
        return own_ref[(tap_x * 3 + tap_y) * 3 + tap_z]

    none = jnp.zeros((chans, total), F32)

    def ahead(r, c):
        return c == ring_device((place + r // rows) % peers, peers) * rows + r % rows

    pick = one_hot((total, total), ahead)
    for ref, taps_x in ((local_ref, (1, 2)), (halo_ref, (0,))):
        tiles = [
            none if tap_y < 0 else tile(tap_x, tap_y, tap_z)
            for taps_y in ((-1, 0), (1, 2))
            for tap_x in taps_x
            for tap_z in range(3)
            for tap_y in taps_y
        ]
        stack = jnp.concatenate(tiles, axis=0).astype(BF16)
        ref[...] = lax.dot_general(
            pick, stack, (((1,), (1,)), ((), ())), preferred_element_type=F32
        ).astype(BF16)

    back = jnp.zeros(back_ref.shape, F32)
    by_offset = ((1, 2), (-1, 0))
    for offset in range(2):
        for plane in range(2):
            tiles = [
                none if min(tap_x, tap_y) < 0 else tile(tap_x, tap_y, tap_z)
                for tap_x in by_offset[plane]
                for tap_z in (1, 2, 0)
                for tap_y in by_offset[offset]
            ]
            stack = jnp.concatenate(tiles, axis=0).astype(BF16)
            first = (offset * 2 + plane) * total

            def behind(r, c, first=first):
                c = c - first
                device = ring_device((place + peers - c // rows) % peers, peers)
                return (r == device * rows + c % rows) & (c >= 0) & (c < total)

            back = back + dot(stack, one_hot((total, 4 * total), behind))
    back_ref[...] = back.astype(BF16)


def call(kernel, name, out_shape, args, scratch=(), flops=0, bytes_accessed=1 << 20, transcendentals=0):
    return pl.pallas_call(
        kernel,
        out_shape=out_shape,
        scratch_shapes=list(scratch),
        compiler_params=PARAMS,
        cost_estimate=pl.CostEstimate(
            flops=flops, bytes_accessed=bytes_accessed, transcendentals=transcendentals
        ),
        name=name,
    )(*args)


def on_device(field, kernel, bias, cotangent):
    peers = lax.axis_size("col")
    me = lax.axis_index("col")
    quarter = peers // 4
    cin, planes, span_y, span_z = field.shape
    cout = bias.shape[0]
    half_y, half_z = span_y // 2, span_z // 2
    counts = (half_y // 2, half_y - half_y // 2)
    starts = (0, counts[0])
    mid = 2 * counts[0]
    last = span_y - ROWS
    plane = lax.optimization_barrier(field[:, planes - 1])
    halos = [jnp.concatenate([plane[:, last:], plane[:, :mid]], axis=1), plane[:, mid:last]]
    halos = [shifted(halo, "gx", 1) for halo in halos]

    chans = -(-cin // 8) * 8
    rows = -(-cout // ROWS) * ROWS
    total = peers * rows
    fill_c = (0, chans - cin)
    fill_o = (0, rows - cout)
    own = lax.dynamic_slice_in_dim(jnp.transpose(kernel, (2, 3, 4, 1, 0)), me * cin, cin, 3)
    own = own.reshape(27, cin, peers, cout)
    own = jnp.pad(own, ((0, 0), fill_c, (0, 0), fill_o)).reshape(27, chans, total)
    own = own.astype(F32)
    field_p = jnp.pad(field, (fill_c, (0, 0), (0, 0), (0, 0)))

    points = half_y * half_z
    vmem = pl.BlockSpec(memory_space=pltpu.VMEM)
    weights_local, weights_halo, weights_back = pl.pallas_call(
        functools.partial(weights_kernel, peers),
        out_shape=[
            jax.ShapeDtypeStruct((total, 24 * chans), BF16),
            jax.ShapeDtypeStruct((total, 12 * chans), BF16),
            jax.ShapeDtypeStruct((12 * chans, 4 * total), BF16),
        ],
        in_specs=[pl.BlockSpec(memory_space=pltpu.SMEM), vmem],
        out_specs=[vmem] * 3,
        compiler_params=PARAMS,
        cost_estimate=pl.CostEstimate(flops=1 << 27, bytes_accessed=1 << 19, transcendentals=0),
        name="weights",
    )(me.astype(jnp.int32).reshape(1), own)
    acc = call(
        local_kernel,
        "local_planes",
        jax.ShapeDtypeStruct((total, points), F32),
        (field_p, weights_local),
        [pltpu.VMEM((planes * 6 * chans, (1 + half_y) * half_z), BF16)],
        flops=2 * total * 24 * chans * points,
        bytes_accessed=1 << 22,
    )
    halos = [jnp.pad(halo, (fill_c, (0, 0), (0, 0))) for halo in halos]
    shapes = [jax.ShapeDtypeStruct((count, rows, half_z), BF16) for count in counts]
    parts = []
    for part in range(2):
        if part:
            weights_halo, parts[0] = lax.optimization_barrier((weights_halo, parts[0]))
        parts.append(
            call(
                functools.partial(halo_kernel, part),
                "halo_plane",
                [shapes[part]] * peers,
                (*halos[: part + 1], weights_halo, acc),
                [pltpu.VMEM((6 * chans, (1 + counts[part]) * half_z), BF16)],
                flops=total * 12 * chans * points,
                bytes_accessed=1 << 21,
            )
        )

    far = 2 * quarter
    steps = (quarter, peers - quarter)
    arrived = [[parts[h][0]] for h in range(2)]
    relayed = [shifted(parts[h][far], "col", steps[h]) for h in range(2)]
    for h in range(2):
        for r in range(1, peers):
            if r not in (steps[h], far):
                sent = parts[h][r]
                if h:
                    sent, relayed[0] = lax.optimization_barrier((sent, relayed[0]))
                arrived[h].append(shifted(sent, "col", r))
    for h in range(2):
        if h:
            relayed[1], arrived[0][-1] = lax.optimization_barrier((relayed[1], arrived[0][-1]))
        joined = call(add_kernel, "add", shapes[h], (relayed[h], parts[h][steps[h]]))
        arrived[h].append(shifted(joined, "col", steps[h]))

    bias_p = jnp.broadcast_to(jnp.pad(bias, fill_o)[None, :, None], (1, rows, half_z))
    cot = jnp.pad(jnp.transpose(cotangent[:, 0], (1, 0, 2)), ((0, 0), fill_o, (0, 0)))
    acts = [
        call(
            act_kernel,
            "activation",
            (shapes[h], shapes[h]),
            (*arrived[h], bias_p, cot[starts[h] : starts[h] + counts[h]]),
            transcendentals=3 * counts[h] * rows * half_z,
        )
        for h in range(2)
    ]
    out = jnp.concatenate([out for out, _ in acts], axis=0)
    out_act = jnp.transpose(out[:, :cout], (1, 0, 2))[:, None]

    masked = [masked for _, masked in acts]
    near = [r for r in range(1, peers) if r != far]
    gathered = [{0: masked[h], **{r: shifted(masked[h], "col", r) for r in near}} for h in range(2)]
    above = [{}, {}]
    arrays = []

    def place_of(value):
        arrays.append(value)
        return len(arrays) - 1

    whole = place_of(shifted(jnp.concatenate(masked, axis=0), "gx", -1))
    for h in range(2):
        above[h][0] = (whole, starts[h])
    gathered[0] = lax.optimization_barrier(gathered[0])
    for h in range(2):
        joined = jnp.concatenate([gathered[h][r] for r in near], axis=0)
        number = place_of(shifted(joined, "gx", -1))
        for i, r in enumerate(near):
            above[h][r] = (number, i * counts[h])
    for h in range(2):
        gathered[h][far] = shifted(gathered[h][steps[h]], "col", steps[h])
        above[h][far] = (place_of(shifted(gathered[h][far], "gx", -1)), 0)
    mine = [{r: (place_of(gathered[h][r]), 0) for r in range(peers)} for h in range(2)]
    order = [[places[h][r] for h in range(2)] for places in (mine, above) for r in range(peers)]

    def grad_call(kernel, name, shape, used, extra, blocks):
        used = sorted(used)
        renamed = [[(used.index(n) if n in used else -1, at) for n, at in both] for both in order]
        return call(
            functools.partial(kernel, renamed),
            name,
            shape,
            (*[arrays[n] for n in used], weights_back, *extra),
            [
                pltpu.VMEM((2 * total, (1 + 8 * blocks) * half_z), BF16),
            ],
            flops=8 * total * 12 * chans * 8 * blocks * half_z,
        )

    done = mid - ROWS
    lower = grad_call(
        lower_grad_kernel,
        "lower_grad",
        jax.ShapeDtypeStruct((chans, planes, done, span_z), BF16),
        {both[0][0] for both in order},
        (),
        done // ROWS,
    )
    in_grad = grad_call(
        lambda pieces, *refs: upper_grad_kernel(pieces, counts, *refs),
        "upper_grad",
        jax.ShapeDtypeStruct((chans, planes, span_y, span_z), BF16),
        {n for both in order for n, _ in both},
        (lower,),
        (span_y - done) // ROWS,
    )
    return out_act, in_grad[:cin]


def solution(mesh):
    in_specs = (P("col", "gx", None, None), P(), P("col"), P("col", "gx", None, None))
    out_specs = (P("col", "gx", None, None), P("col", "gx", None, None))
    return jax.shard_map(
        on_device, mesh=mesh, in_specs=in_specs, out_specs=out_specs, check_vma=False
    )
```

```python
import functools

import jax
import jax.numpy as jnp
from jax import lax
from jax.experimental import pallas as pl
from jax.experimental.pallas import tpu as pltpu
from jax.sharding import PartitionSpec as P

F32 = jnp.float32
BF16 = jnp.bfloat16
LANES = 128
ROWS = 16
PARAMS = pltpu.CompilerParams(vmem_limit_bytes=24 * 1024 * 1024)


def ring_device(place, count):
    return jnp.where(2 * place < count, 2 * place, 2 * (count - place) - 1)


def ring_place(device, count):
    return jnp.where(device % 2 == 0, device // 2, count - (device + 1) // 2)


def shifted(block, axis, distance):
    count = lax.axis_size(axis)
    ring = list(range(count))
    if axis == "col":
        ring = ring[::2] + ring[1::2][::-1]
    return lax.ppermute(block, axis, [(ring[i], ring[(i + distance) % count]) for i in range(count)])


def one_hot(shape, rule):
    rows = lax.broadcasted_iota(jnp.int32, shape, 0)
    cols = lax.broadcasted_iota(jnp.int32, shape, 1)
    return jnp.where(rule(rows, cols), 1.0, 0.0).astype(BF16)


def dot(left, right):
    return jnp.dot(left, right, preferred_element_type=F32)


def fill_taps(blocks, chans, span_z, taps_ref, first_row):
    half_z = span_z // 2
    size = chans * ROWS
    swap = one_hot((size, size), lambda r, c: c == (r % chans) * ROWS + r // chans)
    split = one_hot(
        (span_z, 3 * half_z),
        lambda z, m: z == (2 * (m % half_z) + m // half_z + span_z - 1) % span_z,
    )
    pair = 2 * chans
    beside = jnp.concatenate([values() for values, _, _, _ in blocks], axis=1)
    swapped = dot(swap, beside).astype(BF16)
    below = [swapped[:, i * span_z : (i + 1) * span_z] for i in range(len(blocks))]
    tapped = dot(jnp.concatenate(below, axis=0), split).astype(BF16)
    for index, (_, first, count, place) in enumerate(blocks):
        for j in range(count):
            for tap in range(3):
                source = index * size + (first + j) * pair
                row = first_row + tap * pair
                lane = (place + j) * half_z
                taps_ref[row : row + pair, lane : lane + half_z] = tapped[
                    source : source + pair, tap * half_z : (tap + 1) * half_z
                ]


def rows_of(ref, index, block):
    def values():
        rows = ref[(slice(None), *index, slice(block * ROWS, (block + 1) * ROWS))]
        return rows.reshape(rows.shape[0] * ROWS, rows.shape[-1])

    return values


def tap_sums(weights, taps_ref, lane, width, half_z):
    before = taps_ref[:, lane : lane + width]
    here = taps_ref[:, lane + half_z : lane + half_z + width]
    return dot(weights, jnp.concatenate([before, here], axis=0))


def local_kernel(field_ref, weight_ref, acc_ref, taps_ref):
    chans, planes, span_y, span_z = field_ref.shape
    half_z = span_z // 2
    count = span_y // ROWS
    for plane in range(planes):
        blocks = [(rows_of(field_ref, (plane,), b), 0, 8, 1 + 8 * b) for b in range(count)]
        fill_taps(blocks, chans, span_z, taps_ref, plane * 6 * chans)
    taps_ref[:, :half_z] = taps_ref[:, count * 8 * half_z :]
    weights = weight_ref[...]
    width = 8 * half_z
    for step in range(count):
        lane = step * width
        acc_ref[:, lane : lane + width] = tap_sums(weights, taps_ref, lane, width, half_z)


def halo_kernel(part, *refs):
    halo_refs, (weight_ref, acc_ref), part_refs, taps_ref = (
        refs[: part + 1],
        refs[part + 1 : part + 3],
        refs[part + 3 : -1],
        refs[-1],
    )
    chans, _, span_z = halo_refs[0].shape
    half_z = span_z // 2
    lower = halo_refs[0].shape[1] // ROWS - 1
    if part == 0:
        blocks = [(rows_of(halo_refs[0], (), 0), 7, 1, 0)]
        blocks += [(rows_of(halo_refs[0], (), 1 + b), 0, 8, 1 + 8 * b) for b in range(lower)]
    else:
        upper = halo_refs[1].shape[1] // ROWS
        blocks = [(rows_of(halo_refs[0], (), lower), 7, 1, 0)]
        blocks += [(rows_of(halo_refs[1], (), b), 0, 8, 1 + 8 * b) for b in range(upper)]
        blocks += [(rows_of(halo_refs[0], (), 0), 0, 8, 1 + 8 * upper)]
    fill_taps(blocks, chans, span_z, taps_ref, 0)
    weights = weight_ref[...]
    rows = part_refs[0].shape[0]
    count = part_refs[0].shape[1] // half_z
    width = 8 * half_z
    base = part * (acc_ref.shape[1] - count * half_z)
    for step in range(count // 8):
        lane = step * width
        sums = acc_ref[:, base + lane : base + lane + width]
        sums = (sums + tap_sums(weights, taps_ref, lane, width, half_z)).astype(BF16)
        for peer, ref in enumerate(part_refs):
            ref[:, lane : lane + width] = sums[peer * rows : (peer + 1) * rows]


def add_kernel(one_ref, two_ref, sum_ref):
    sum_ref[...] = (one_ref[...].astype(F32) + two_ref[...].astype(F32)).astype(BF16)


def act_kernel(*refs):
    *part_refs, bias_ref, cot_ref, out_ref, masked_ref = refs
    pre = bias_ref[...] + functools.reduce(
        lambda a, b: a + b, [ref[...].astype(F32) for ref in part_refs]
    )
    small = jnp.exp(-jnp.abs(pre))
    soft = jnp.maximum(pre, 0.0) + jnp.log(1.0 + small)
    out_ref[...] = (0.3 * pre + 0.7 * soft).astype(BF16)
    gate = jnp.where(pre >= 0.0, 1.0, small) / (1.0 + small)
    masked_ref[...] = (cot_ref[...].astype(F32) * (0.3 + 0.7 * gate)).astype(BF16)


def grad_blocks(here, after, weights, blocks, chans, span_z, store):
    half_z = span_z // 2
    size = chans * ROWS
    swap = one_hot((size, size), lambda r, c: c == (r % ROWS) * chans + r // ROWS)
    weave = one_hot((span_z, span_z), lambda m, z: z == 2 * (m % half_z) + m // half_z)
    pair = 2 * chans
    sums = dot(weights, jnp.concatenate(here + after, axis=0))
    beside = []
    for step in range(blocks):
        for parity_x in range(2):
            base = parity_x * 3 * pair
            rows = []
            for j in range(step * 8, step * 8 + 8):
                tile = sums[base : base + 3 * pair, j * half_z : (j + 1) * half_z]
                even = tile[:pair]
                odd = tile[pair : 2 * pair] + pltpu.roll(tile[2 * pair :], half_z - 1, 1)
                rows.append(jnp.concatenate([even.astype(BF16), odd.astype(BF16)], axis=1))
            beside.append(jnp.concatenate(rows, axis=0))
    swapped = dot(swap, jnp.concatenate(beside, axis=1)).astype(BF16)
    below = [swapped[:, i * span_z : (i + 1) * span_z] for i in range(2 * blocks)]
    woven = dot(jnp.concatenate(below, axis=0), weave).astype(BF16)
    for step in range(blocks):
        for parity_x in range(2):
            for chan in range(chans):
                first = (step * 2 + parity_x) * size + chan * ROWS
                store(chan, parity_x, step, woven[first : first + ROWS])


def lanes_of(ref, at, first, last):
    row, lane = at
    return ref[row : row + ROWS, lane + first : lane + last]


def lower_grad_kernel(pieces, *refs):
    *piece_refs, weight_ref, grad_ref = refs
    chans, _, span_y, span_z = grad_ref.shape
    half_z = span_z // 2
    width = span_y // 2 * half_z
    low = [(piece_refs[number], at) for (number, at), _ in pieces]
    here = [lanes_of(*piece, 0, width) for piece in low]
    after = [lanes_of(*piece, half_z, half_z + width) for piece in low]

    def store(chan, parity_x, step, values):
        grad_ref[chan, parity_x, step * ROWS : (step + 1) * ROWS, :] = values

    grad_blocks(here, after, weight_ref[...], span_y // ROWS, chans, span_z, store)


def upper_grad_kernel(pieces, counts, *refs):
    *piece_refs, weight_ref, lower_ref, grad_ref = refs
    chans, _, span_y, span_z = grad_ref.shape
    half_z = span_z // 2
    done = lower_ref.shape[2]
    grad_ref[:, :, :done, :] = lower_ref[...]
    first, low_end, high_end = done // 2 * half_z, counts[0] * half_z, counts[1] * half_z
    here, after = [], []
    for (low, low_at), (high, high_at) in pieces:
        upper = lanes_of(piece_refs[high], high_at, 0, high_end)
        low_ref = piece_refs[low]
        here.append(jnp.concatenate([lanes_of(low_ref, low_at, first, low_end), upper], axis=1))
        rest = lanes_of(low_ref, low_at, first + half_z, low_end)
        wrapped = lanes_of(low_ref, low_at, 0, half_z)
        after.append(jnp.concatenate([rest, upper, wrapped], axis=1))

    def store(chan, parity_x, step, values):
        place = done + step * ROWS
        grad_ref[chan, parity_x, place : place + ROWS, :] = values

    grad_blocks(here, after, weight_ref[...], (span_y - done) // ROWS, chans, span_z, store)


def weights_kernel(peers, me_ref, own_ref, local_ref, halo_ref, back_ref):
    _, chans, total = own_ref.shape
    rows = total // peers
    place = ring_place(me_ref[0], peers)

    def tile(tap_x, tap_y, tap_z):
        return own_ref[(tap_x * 3 + tap_y) * 3 + tap_z]

    none = jnp.zeros((chans, total), F32)

    def ahead(r, c):
        return c == ring_device((place + r // rows) % peers, peers) * rows + r % rows

    pick = one_hot((total, total), ahead)
    for ref, taps_x in ((local_ref, (1, 2)), (halo_ref, (0,))):
        tiles = [
            none if tap_y < 0 else tile(tap_x, tap_y, tap_z)
            for taps_y in ((-1, 0), (1, 2))
            for tap_x in taps_x
            for tap_z in range(3)
            for tap_y in taps_y
        ]
        stack = jnp.concatenate(tiles, axis=0).astype(BF16)
        ref[...] = lax.dot_general(
            pick, stack, (((1,), (1,)), ((), ())), preferred_element_type=F32
        ).astype(BF16)

    back = jnp.zeros(back_ref.shape, F32)
    by_offset = ((1, 2), (-1, 0))
    for offset in range(2):
        for plane in range(2):
            tiles = [
                none if min(tap_x, tap_y) < 0 else tile(tap_x, tap_y, tap_z)
                for tap_x in by_offset[plane]
                for tap_z in (1, 2, 0)
                for tap_y in by_offset[offset]
            ]
            stack = jnp.concatenate(tiles, axis=0).astype(BF16)
            first = (offset * 2 + plane) * total

            def behind(r, c, first=first):
                c = c - first
                device = ring_device((place + peers - c // rows) % peers, peers)
                return (r == device * rows + c % rows) & (c >= 0) & (c < total)

            back = back + dot(stack, one_hot((total, 4 * total), behind))
    back_ref[...] = back.astype(BF16)


def call(kernel, name, out_shape, args, scratch=(), flops=0, bytes_accessed=1 << 20, transcendentals=0):
    return pl.pallas_call(
        kernel,
        out_shape=out_shape,
        scratch_shapes=list(scratch),
        compiler_params=PARAMS,
        cost_estimate=pl.CostEstimate(
            flops=flops, bytes_accessed=bytes_accessed, transcendentals=transcendentals
        ),
        name=name,
    )(*args)


def on_device(field, kernel, bias, cotangent):
    peers = lax.axis_size("col")
    me = lax.axis_index("col")
    quarter = peers // 4
    cin, planes, span_y, span_z = field.shape
    cout = bias.shape[0]
    half_y, half_z = span_y // 2, span_z // 2
    counts = (half_y // 2, half_y - half_y // 2)
    starts = (0, counts[0])
    mid = 2 * counts[0]
    last = span_y - ROWS
    plane = lax.optimization_barrier(field[:, planes - 1])
    halos = [jnp.concatenate([plane[:, last:], plane[:, :mid]], axis=1), plane[:, mid:last]]
    halos = [shifted(halo, "gx", 1) for halo in halos]

    chans = -(-cin // 8) * 8
    rows = -(-cout // ROWS) * ROWS
    total = peers * rows
    fill_c = (0, chans - cin)
    fill_o = (0, rows - cout)
    own = lax.dynamic_slice_in_dim(jnp.transpose(kernel, (2, 3, 4, 1, 0)), me * cin, cin, 3)
    own = own.reshape(27, cin, peers, cout)
    own = jnp.pad(own, ((0, 0), fill_c, (0, 0), fill_o)).reshape(27, chans, total)
    own = own.astype(F32)
    field_p = jnp.pad(field, (fill_c, (0, 0), (0, 0), (0, 0)))

    points = half_y * half_z
    vmem = pl.BlockSpec(memory_space=pltpu.VMEM)
    weights_local, weights_halo, weights_back = pl.pallas_call(
        functools.partial(weights_kernel, peers),
        out_shape=[
            jax.ShapeDtypeStruct((total, 24 * chans), BF16),
            jax.ShapeDtypeStruct((total, 12 * chans), BF16),
            jax.ShapeDtypeStruct((12 * chans, 4 * total), BF16),
        ],
        in_specs=[pl.BlockSpec(memory_space=pltpu.SMEM), vmem],
        out_specs=[vmem] * 3,
        compiler_params=PARAMS,
        cost_estimate=pl.CostEstimate(flops=1 << 27, bytes_accessed=1 << 19, transcendentals=0),
        name="weights",
    )(me.astype(jnp.int32).reshape(1), own)
    acc = call(
        local_kernel,
        "local_planes",
        jax.ShapeDtypeStruct((total, points), F32),
        (field_p, weights_local),
        [pltpu.VMEM((planes * 6 * chans, (1 + half_y) * half_z), BF16)],
        flops=2 * total * 24 * chans * points,
        bytes_accessed=1 << 22,
    )
    halos = [jnp.pad(halo, (fill_c, (0, 0), (0, 0))) for halo in halos]
    shapes = [jax.ShapeDtypeStruct((rows, count * half_z), BF16) for count in counts]
    parts = []
    for part in range(2):
        if part:
            weights_halo, parts[0] = lax.optimization_barrier((weights_halo, parts[0]))
        parts.append(
            call(
                functools.partial(halo_kernel, part),
                "halo_plane",
                [shapes[part]] * peers,
                (*halos[: part + 1], weights_halo, acc),
                [pltpu.VMEM((6 * chans, (1 + counts[part]) * half_z), BF16)],
                flops=total * 12 * chans * points,
                bytes_accessed=1 << 21,
            )
        )

    far = 2 * quarter
    steps = (quarter, peers - quarter)
    arrived = [[parts[h][0]] for h in range(2)]
    relayed = [shifted(parts[h][far], "col", steps[h]) for h in range(2)]
    for h in range(2):
        for r in range(1, peers):
            if r not in (steps[h], far):
                sent = parts[h][r]
                if h:
                    sent, relayed[0] = lax.optimization_barrier((sent, relayed[0]))
                arrived[h].append(shifted(sent, "col", r))
    for h in range(2):
        if h:
            relayed[1], arrived[0][-1] = lax.optimization_barrier((relayed[1], arrived[0][-1]))
        joined = call(add_kernel, "add", shapes[h], (relayed[h], parts[h][steps[h]]))
        arrived[h].append(shifted(joined, "col", steps[h]))

    bias_p = [jnp.broadcast_to(jnp.pad(bias, fill_o)[:, None], shape.shape) for shape in shapes]
    cot = jnp.pad(cotangent.reshape(cout, points), (fill_o, (0, 0)))
    acts = [
        call(
            act_kernel,
            "activation",
            (shapes[h], shapes[h]),
            (*arrived[h], bias_p[h], cot[:, starts[h] * half_z : (starts[h] + counts[h]) * half_z]),
            transcendentals=3 * counts[h] * rows * half_z,
        )
        for h in range(2)
    ]
    out = jnp.concatenate([out for out, _ in acts], axis=1)
    out_act = out[:cout].reshape(cout, 1, half_y, half_z)

    masked = [masked for _, masked in acts]
    near = [r for r in range(1, peers) if r != far]
    gathered = [{0: masked[h], **{r: shifted(masked[h], "col", r) for r in near}} for h in range(2)]
    above = [{}, {}]
    arrays = []

    def place_of(value):
        arrays.append(value)
        return len(arrays) - 1

    whole = place_of(shifted(jnp.concatenate(masked, axis=1), "gx", -1))
    for h in range(2):
        above[h][0] = (whole, (0, starts[h] * half_z))
    gathered[0] = lax.optimization_barrier(gathered[0])
    for h in range(2):
        joined = jnp.concatenate([gathered[h][r] for r in near], axis=0)
        number = place_of(shifted(joined, "gx", -1))
        for i, r in enumerate(near):
            above[h][r] = (number, (i * rows, 0))
    for h in range(2):
        gathered[h][far] = shifted(gathered[h][steps[h]], "col", steps[h])
        above[h][far] = (place_of(shifted(gathered[h][far], "gx", -1)), (0, 0))
    mine = [{r: (place_of(gathered[h][r]), (0, 0)) for r in range(peers)} for h in range(2)]
    order = [[places[h][r] for h in range(2)] for places in (mine, above) for r in range(peers)]

    def grad_call(kernel, name, shape, used, extra, blocks):
        used = sorted(used)
        renamed = [[(used.index(n) if n in used else -1, at) for n, at in both] for both in order]
        return call(
            functools.partial(kernel, renamed),
            name,
            shape,
            (*[arrays[n] for n in used], weights_back, *extra),
            flops=8 * total * 12 * chans * 8 * blocks * half_z,
        )

    done = mid - ROWS
    lower = grad_call(
        lower_grad_kernel,
        "lower_grad",
        jax.ShapeDtypeStruct((chans, planes, done, span_z), BF16),
        {both[0][0] for both in order},
        (),
        done // ROWS,
    )
    in_grad = grad_call(
        lambda pieces, *refs: upper_grad_kernel(pieces, counts, *refs),
        "upper_grad",
        jax.ShapeDtypeStruct((chans, planes, span_y, span_z), BF16),
        {n for both in order for n, _ in both},
        (lower,),
        (span_y - done) // ROWS,
    )
    return out_act, in_grad[:cin]


def solution(mesh):
    in_specs = (P("col", "gx", None, None), P(), P("col"), P("col", "gx", None, None))
    out_specs = (P("col", "gx", None, None), P("col", "gx", None, None))
    return jax.shard_map(
        on_device, mesh=mesh, in_specs=in_specs, out_specs=out_specs, check_vma=False
    )
```

```python
import functools

import jax
import jax.numpy as jnp
from jax import lax
from jax.experimental import pallas as pl
from jax.experimental.pallas import tpu as pltpu
from jax.sharding import PartitionSpec as P

F32 = jnp.float32
BF16 = jnp.bfloat16
LANES = 128
ROWS = 16
PARAMS = pltpu.CompilerParams(vmem_limit_bytes=24 * 1024 * 1024)


def ring_device(place, count):
    return jnp.where(2 * place < count, 2 * place, 2 * (count - place) - 1)


def ring_place(device, count):
    return jnp.where(device % 2 == 0, device // 2, count - (device + 1) // 2)


def shifted(block, axis, distance):
    count = lax.axis_size(axis)
    ring = list(range(count))
    if axis == "col":
        ring = ring[::2] + ring[1::2][::-1]
    return lax.ppermute(block, axis, [(ring[i], ring[(i + distance) % count]) for i in range(count)])


def one_hot(shape, rule):
    rows = lax.broadcasted_iota(jnp.int32, shape, 0)
    cols = lax.broadcasted_iota(jnp.int32, shape, 1)
    return jnp.where(rule(rows, cols), 1.0, 0.0).astype(BF16)


def dot(left, right):
    return jnp.dot(left, right, preferred_element_type=F32)


def fill_taps(blocks, chans, span_z, taps_ref, first_row):
    half_z = span_z // 2
    size = chans * ROWS
    swap = one_hot((size, size), lambda r, c: c == (r % chans) * ROWS + r // chans)
    split = one_hot(
        (span_z, 3 * half_z),
        lambda z, m: z == (2 * (m % half_z) + m // half_z + span_z - 1) % span_z,
    )
    pair = 2 * chans
    beside = jnp.concatenate([values() for values, _, _, _ in blocks], axis=1)
    swapped = dot(swap, beside).astype(BF16)
    below = [swapped[:, i * span_z : (i + 1) * span_z] for i in range(len(blocks))]
    tapped = dot(jnp.concatenate(below, axis=0), split).astype(BF16)
    for index, (_, first, count, place) in enumerate(blocks):
        for j in range(count):
            for tap in range(3):
                source = index * size + (first + j) * pair
                row = first_row + tap * pair
                lane = (place + j) * half_z
                taps_ref[row : row + pair, lane : lane + half_z] = tapped[
                    source : source + pair, tap * half_z : (tap + 1) * half_z
                ]


def rows_of(ref, index, block):
    def values():
        rows = ref[(slice(None), *index, slice(block * ROWS, (block + 1) * ROWS))]
        return rows.reshape(rows.shape[0] * ROWS, rows.shape[-1])

    return values


def tap_sums(weights, taps_ref, lane, width, half_z):
    before = taps_ref[:, lane : lane + width]
    here = taps_ref[:, lane + half_z : lane + half_z + width]
    return dot(weights, jnp.concatenate([before, here], axis=0))


def local_kernel(field_ref, weight_ref, acc_ref, taps_ref):
    chans, planes, span_y, span_z = field_ref.shape
    half_z = span_z // 2
    count = span_y // ROWS
    for plane in range(planes):
        blocks = [(rows_of(field_ref, (plane,), b), 0, 8, 1 + 8 * b) for b in range(count)]
        fill_taps(blocks, chans, span_z, taps_ref, plane * 6 * chans)
    taps_ref[:, :half_z] = taps_ref[:, count * 8 * half_z :]
    weights = weight_ref[...]
    width = 8 * half_z
    for step in range(count):
        lane = step * width
        acc_ref[:, lane : lane + width] = tap_sums(weights, taps_ref, lane, width, half_z)


def halo_kernel(part, *refs):
    halo_refs, (weight_ref, acc_ref), part_refs, taps_ref = (
        refs[: part + 1],
        refs[part + 1 : part + 3],
        refs[part + 3 : -1],
        refs[-1],
    )
    chans, _, span_z = halo_refs[0].shape
    half_z = span_z // 2
    lower = halo_refs[0].shape[1] // ROWS - 1
    if part == 0:
        blocks = [(rows_of(halo_refs[0], (), 0), 7, 1, 0)]
        blocks += [(rows_of(halo_refs[0], (), 1 + b), 0, 8, 1 + 8 * b) for b in range(lower)]
    else:
        upper = halo_refs[1].shape[1] // ROWS
        blocks = [(rows_of(halo_refs[0], (), lower), 7, 1, 0)]
        blocks += [(rows_of(halo_refs[1], (), b), 0, 8, 1 + 8 * b) for b in range(upper)]
        blocks += [(rows_of(halo_refs[0], (), 0), 0, 8, 1 + 8 * upper)]
    fill_taps(blocks, chans, span_z, taps_ref, 0)
    weights = weight_ref[...]
    rows = part_refs[0].shape[0]
    count = part_refs[0].shape[1] // half_z
    width = 8 * half_z
    base = part * (acc_ref.shape[1] - count * half_z)
    for step in range(count // 8):
        lane = step * width
        sums = acc_ref[:, base + lane : base + lane + width]
        sums = (sums + tap_sums(weights, taps_ref, lane, width, half_z)).astype(BF16)
        for peer, ref in enumerate(part_refs):
            ref[:, lane : lane + width] = sums[peer * rows : (peer + 1) * rows]


def add_kernel(one_ref, two_ref, sum_ref):
    sum_ref[...] = (one_ref[...].astype(F32) + two_ref[...].astype(F32)).astype(BF16)


def act_kernel(*refs):
    *part_refs, bias_ref, cot_ref, out_ref, masked_ref = refs
    pre = bias_ref[...] + functools.reduce(
        lambda a, b: a + b, [ref[...].astype(F32) for ref in part_refs]
    )
    small = jnp.exp(-jnp.abs(pre))
    soft = jnp.maximum(pre, 0.0) + jnp.log(1.0 + small)
    out_ref[...] = (0.3 * pre + 0.7 * soft).astype(BF16)
    gate = jnp.where(pre >= 0.0, 1.0, small) / (1.0 + small)
    masked_ref[...] = (cot_ref[...].astype(F32) * (0.3 + 0.7 * gate)).astype(BF16)


def grad_blocks(here, after, weights, blocks, chans, span_z, store):
    half_z = span_z // 2
    size = chans * ROWS
    swap = one_hot((size, size), lambda r, c: c == (r % ROWS) * chans + r // ROWS)
    weave = one_hot((span_z, span_z), lambda m, z: z == 2 * (m % half_z) + m // half_z)
    pair = 2 * chans
    sums = dot(weights, jnp.concatenate(here + after, axis=0))
    beside = []
    for step in range(blocks):
        for parity_x in range(2):
            base = parity_x * 3 * pair
            rows = []
            for j in range(step * 8, step * 8 + 8):
                tile = sums[base : base + 3 * pair, j * half_z : (j + 1) * half_z]
                even = tile[:pair]
                odd = tile[pair : 2 * pair] + pltpu.roll(tile[2 * pair :], half_z - 1, 1)
                rows.append(jnp.concatenate([even.astype(BF16), odd.astype(BF16)], axis=1))
            beside.append(jnp.concatenate(rows, axis=0))
    swapped = dot(swap, jnp.concatenate(beside, axis=1)).astype(BF16)
    below = [swapped[:, i * span_z : (i + 1) * span_z] for i in range(2 * blocks)]
    woven = dot(jnp.concatenate(below, axis=0), weave).astype(BF16)
    for step in range(blocks):
        for parity_x in range(2):
            for chan in range(chans):
                first = (step * 2 + parity_x) * size + chan * ROWS
                store(chan, parity_x, step, woven[first : first + ROWS])


def lanes_of(ref, at, first, last):
    row, lane = at
    return ref[row : row + ROWS, lane + first : lane + last]


def lower_grad_kernel(pieces, *refs):
    *piece_refs, weight_ref, grad_ref = refs
    chans, _, span_y, span_z = grad_ref.shape
    half_z = span_z // 2
    width = span_y // 2 * half_z
    low = [(piece_refs[number], at) for (number, at), _ in pieces]
    here = [lanes_of(*piece, 0, width) for piece in low]
    after = [lanes_of(*piece, half_z, half_z + width) for piece in low]

    def store(chan, parity_x, step, values):
        grad_ref[chan, parity_x, step * ROWS : (step + 1) * ROWS, :] = values

    grad_blocks(here, after, weight_ref[...], span_y // ROWS, chans, span_z, store)


def upper_grad_kernel(pieces, counts, *refs):
    *piece_refs, weight_ref, lower_ref, grad_ref, stage_ref, sems = refs
    chans, _, span_y, span_z = grad_ref.shape
    half_z = span_z // 2
    done = lower_ref.shape[2]
    lower_copy = pltpu.make_async_copy(lower_ref, grad_ref.at[:, :, pl.ds(0, done)], sems.at[0])
    lower_copy.start()
    first, low_end, high_end = done // 2 * half_z, counts[0] * half_z, counts[1] * half_z
    here, after = [], []
    for (low, low_at), (high, high_at) in pieces:
        upper = lanes_of(piece_refs[high], high_at, 0, high_end)
        low_ref = piece_refs[low]
        here.append(jnp.concatenate([lanes_of(low_ref, low_at, first, low_end), upper], axis=1))
        rest = lanes_of(low_ref, low_at, first + half_z, low_end)
        wrapped = lanes_of(low_ref, low_at, 0, half_z)
        after.append(jnp.concatenate([rest, upper, wrapped], axis=1))

    def store(chan, parity_x, step, values):
        stage_ref[chan, parity_x, step * ROWS : (step + 1) * ROWS, :] = values

    grad_blocks(here, after, weight_ref[...], (span_y - done) // ROWS, chans, span_z, store)
    upper_rows = pl.ds(done, span_y - done)
    upper_copy = pltpu.make_async_copy(stage_ref, grad_ref.at[:, :, upper_rows], sems.at[1])
    upper_copy.start()
    lower_copy.wait()
    upper_copy.wait()


def weights_kernel(peers, me_ref, own_ref, local_ref, halo_ref, back_ref):
    _, chans, total = own_ref.shape
    rows = total // peers
    place = ring_place(me_ref[0], peers)

    def tile(tap_x, tap_y, tap_z):
        return own_ref[(tap_x * 3 + tap_y) * 3 + tap_z]

    none = jnp.zeros((chans, total), F32)

    def ahead(r, c):
        return c == ring_device((place + r // rows) % peers, peers) * rows + r % rows

    pick = one_hot((total, total), ahead)
    for ref, taps_x in ((local_ref, (1, 2)), (halo_ref, (0,))):
        tiles = [
            none if tap_y < 0 else tile(tap_x, tap_y, tap_z)
            for taps_y in ((-1, 0), (1, 2))
            for tap_x in taps_x
            for tap_z in range(3)
            for tap_y in taps_y
        ]
        stack = jnp.concatenate(tiles, axis=0).astype(BF16)
        ref[...] = lax.dot_general(
            pick, stack, (((1,), (1,)), ((), ())), preferred_element_type=F32
        ).astype(BF16)

    back = jnp.zeros(back_ref.shape, F32)
    by_offset = ((1, 2), (-1, 0))
    for offset in range(2):
        for plane in range(2):
            tiles = [
                none if min(tap_x, tap_y) < 0 else tile(tap_x, tap_y, tap_z)
                for tap_x in by_offset[plane]
                for tap_z in (1, 2, 0)
                for tap_y in by_offset[offset]
            ]
            stack = jnp.concatenate(tiles, axis=0).astype(BF16)
            first = (offset * 2 + plane) * total

            def behind(r, c, first=first):
                c = c - first
                device = ring_device((place + peers - c // rows) % peers, peers)
                return (r == device * rows + c % rows) & (c >= 0) & (c < total)

            back = back + dot(stack, one_hot((total, 4 * total), behind))
    back_ref[...] = back.astype(BF16)


def call(kernel, name, out_shape, args, scratch=(), flops=0, bytes_accessed=1 << 20, transcendentals=0):
    return pl.pallas_call(
        kernel,
        out_shape=out_shape,
        scratch_shapes=list(scratch),
        compiler_params=PARAMS,
        cost_estimate=pl.CostEstimate(
            flops=flops, bytes_accessed=bytes_accessed, transcendentals=transcendentals
        ),
        name=name,
    )(*args)


def on_device(field, kernel, bias, cotangent):
    peers = lax.axis_size("col")
    me = lax.axis_index("col")
    quarter = peers // 4
    cin, planes, span_y, span_z = field.shape
    cout = bias.shape[0]
    half_y, half_z = span_y // 2, span_z // 2
    counts = (half_y // 2, half_y - half_y // 2)
    starts = (0, counts[0])
    mid = 2 * counts[0]
    last = span_y - ROWS
    plane = lax.optimization_barrier(field[:, planes - 1])
    halos = [jnp.concatenate([plane[:, last:], plane[:, :mid]], axis=1), plane[:, mid:last]]
    halos = [shifted(halo, "gx", 1) for halo in halos]

    chans = -(-cin // 8) * 8
    rows = -(-cout // ROWS) * ROWS
    total = peers * rows
    fill_c = (0, chans - cin)
    fill_o = (0, rows - cout)
    own = lax.dynamic_slice_in_dim(jnp.transpose(kernel, (2, 3, 4, 1, 0)), me * cin, cin, 3)
    own = own.reshape(27, cin, peers, cout)
    own = jnp.pad(own, ((0, 0), fill_c, (0, 0), fill_o)).reshape(27, chans, total)
    own = own.astype(F32)
    field_p = jnp.pad(field, (fill_c, (0, 0), (0, 0), (0, 0)))

    points = half_y * half_z
    vmem = pl.BlockSpec(memory_space=pltpu.VMEM)
    weights_local, weights_halo, weights_back = pl.pallas_call(
        functools.partial(weights_kernel, peers),
        out_shape=[
            jax.ShapeDtypeStruct((total, 24 * chans), BF16),
            jax.ShapeDtypeStruct((total, 12 * chans), BF16),
            jax.ShapeDtypeStruct((12 * chans, 4 * total), BF16),
        ],
        in_specs=[pl.BlockSpec(memory_space=pltpu.SMEM), vmem],
        out_specs=[vmem] * 3,
        compiler_params=PARAMS,
        cost_estimate=pl.CostEstimate(flops=1 << 27, bytes_accessed=1 << 19, transcendentals=0),
        name="weights",
    )(me.astype(jnp.int32).reshape(1), own)
    acc = call(
        local_kernel,
        "local_planes",
        jax.ShapeDtypeStruct((total, points), F32),
        (field_p, weights_local),
        [pltpu.VMEM((planes * 6 * chans, (1 + half_y) * half_z), BF16)],
        flops=2 * total * 24 * chans * points,
        bytes_accessed=1 << 22,
    )
    halos = [jnp.pad(halo, (fill_c, (0, 0), (0, 0))) for halo in halos]
    shapes = [jax.ShapeDtypeStruct((rows, count * half_z), BF16) for count in counts]
    parts = []
    for part in range(2):
        if part:
            weights_halo, parts[0] = lax.optimization_barrier((weights_halo, parts[0]))
        parts.append(
            call(
                functools.partial(halo_kernel, part),
                "halo_plane",
                [shapes[part]] * peers,
                (*halos[: part + 1], weights_halo, acc),
                [pltpu.VMEM((6 * chans, (1 + counts[part]) * half_z), BF16)],
                flops=total * 12 * chans * points,
                bytes_accessed=1 << 21,
            )
        )

    far = 2 * quarter
    steps = (quarter, peers - quarter)
    arrived = [[parts[h][0]] for h in range(2)]
    relayed = [shifted(parts[h][far], "col", steps[h]) for h in range(2)]
    for h in range(2):
        for r in range(1, peers):
            if r not in (steps[h], far):
                sent = parts[h][r]
                if h:
                    sent, relayed[0] = lax.optimization_barrier((sent, relayed[0]))
                arrived[h].append(shifted(sent, "col", r))
    for h in range(2):
        if h:
            relayed[1], arrived[0][-1] = lax.optimization_barrier((relayed[1], arrived[0][-1]))
        joined = call(add_kernel, "add", shapes[h], (relayed[h], parts[h][steps[h]]))
        arrived[h].append(shifted(joined, "col", steps[h]))

    bias_p = [jnp.broadcast_to(jnp.pad(bias, fill_o)[:, None], shape.shape) for shape in shapes]
    cot = jnp.pad(cotangent.reshape(cout, points), (fill_o, (0, 0)))
    acts = [
        call(
            act_kernel,
            "activation",
            (shapes[h], shapes[h]),
            (*arrived[h], bias_p[h], cot[:, starts[h] * half_z : (starts[h] + counts[h]) * half_z]),
            transcendentals=3 * counts[h] * rows * half_z,
        )
        for h in range(2)
    ]
    out = jnp.concatenate([out for out, _ in acts], axis=1)
    out_act = out[:cout].reshape(cout, 1, half_y, half_z)

    masked = [masked for _, masked in acts]
    near = [r for r in range(1, peers) if r != far]
    gathered = [{0: masked[h], **{r: shifted(masked[h], "col", r) for r in near}} for h in range(2)]
    above = [{}, {}]
    arrays = []

    def place_of(value):
        arrays.append(value)
        return len(arrays) - 1

    whole = place_of(shifted(jnp.concatenate(masked, axis=1), "gx", -1))
    for h in range(2):
        above[h][0] = (whole, (0, starts[h] * half_z))
    gathered[0] = lax.optimization_barrier(gathered[0])
    for h in range(2):
        joined = jnp.concatenate([gathered[h][r] for r in near], axis=0)
        number = place_of(shifted(joined, "gx", -1))
        for i, r in enumerate(near):
            above[h][r] = (number, (i * rows, 0))
    for h in range(2):
        gathered[h][far] = shifted(gathered[h][steps[h]], "col", steps[h])
        above[h][far] = (place_of(shifted(gathered[h][far], "gx", -1)), (0, 0))
    mine = [{r: (place_of(gathered[h][r]), (0, 0)) for r in range(peers)} for h in range(2)]
    order = [[places[h][r] for h in range(2)] for places in (mine, above) for r in range(peers)]

    def grad_call(kernel, name, shape, used, extra, blocks):
        used = sorted(used)
        renamed = [[(used.index(n) if n in used else -1, at) for n, at in both] for both in order]
        return call(
            functools.partial(kernel, renamed),
            name,
            shape,
            (*[arrays[n] for n in used], weights_back, *extra),
            flops=8 * total * 12 * chans * 8 * blocks * half_z,
        )

    done = mid - ROWS
    lower = grad_call(
        lower_grad_kernel,
        "lower_grad",
        jax.ShapeDtypeStruct((chans, planes, done, span_z), BF16),
        {both[0][0] for both in order},
        (),
        done // ROWS,
    )
    used = sorted({n for both in order for n, _ in both})
    renamed = [[(used.index(n), at) for n, at in both] for both in order]
    in_grad = pl.pallas_call(
        functools.partial(upper_grad_kernel, renamed, counts),
        out_shape=jax.ShapeDtypeStruct((chans, planes, span_y, span_z), BF16),
        in_specs=[vmem] * (len(used) + 2),
        out_specs=pl.BlockSpec(memory_space=pl.ANY),
        scratch_shapes=[
            pltpu.VMEM((chans, planes, span_y - done, span_z), BF16),
            pltpu.SemaphoreType.DMA((2,)),
        ],
        compiler_params=PARAMS,
        cost_estimate=pl.CostEstimate(
            flops=4 * total * 12 * chans * (span_y - done) * half_z,
            bytes_accessed=1 << 20,
            transcendentals=0,
        ),
        name="upper_grad",
    )(*[arrays[n] for n in used], weights_back, lower)
    return out_act, in_grad[:cin]


def solution(mesh):
    in_specs = (P("col", "gx", None, None), P(), P("col"), P("col", "gx", None, None))
    out_specs = (P("col", "gx", None, None), P("col", "gx", None, None))
    return jax.shard_map(
        on_device, mesh=mesh, in_specs=in_specs, out_specs=out_specs, check_vma=False
    )
```

```python
import functools

import jax
import jax.numpy as jnp
from jax import lax
from jax.experimental import pallas as pl
from jax.experimental.pallas import tpu as pltpu
from jax.sharding import PartitionSpec as P

F32 = jnp.float32
BF16 = jnp.bfloat16
LANES = 128
ROWS = 16
PARAMS = pltpu.CompilerParams(vmem_limit_bytes=24 * 1024 * 1024)


def ring_device(place, count):
    return jnp.where(2 * place < count, 2 * place, 2 * (count - place) - 1)


def ring_place(device, count):
    return jnp.where(device % 2 == 0, device // 2, count - (device + 1) // 2)


def shifted(block, axis, distance):
    count = lax.axis_size(axis)
    ring = list(range(count))
    if axis == "col":
        ring = ring[::2] + ring[1::2][::-1]
    return lax.ppermute(block, axis, [(ring[i], ring[(i + distance) % count]) for i in range(count)])


def one_hot(shape, rule):
    rows = lax.broadcasted_iota(jnp.int32, shape, 0)
    cols = lax.broadcasted_iota(jnp.int32, shape, 1)
    return jnp.where(rule(rows, cols), 1.0, 0.0).astype(BF16)


def dot(left, right):
    return jnp.dot(left, right, preferred_element_type=F32)


def fill_taps(blocks, chans, span_z, taps_ref, first_row):
    half_z = span_z // 2
    size = chans * ROWS
    swap = one_hot((size, size), lambda r, c: c == (r % chans) * ROWS + r // chans)
    split = one_hot(
        (span_z, 3 * half_z),
        lambda z, m: z == (2 * (m % half_z) + m // half_z + span_z - 1) % span_z,
    )
    pair = 2 * chans
    beside = jnp.concatenate([values() for values, _, _, _ in blocks], axis=1)
    swapped = dot(swap, beside).astype(BF16)
    below = [swapped[:, i * span_z : (i + 1) * span_z] for i in range(len(blocks))]
    tapped = dot(jnp.concatenate(below, axis=0), split).astype(BF16)
    for index, (_, first, count, place) in enumerate(blocks):
        for j in range(count):
            for tap in range(3):
                source = index * size + (first + j) * pair
                row = first_row + tap * pair
                lane = (place + j) * half_z
                taps_ref[row : row + pair, lane : lane + half_z] = tapped[
                    source : source + pair, tap * half_z : (tap + 1) * half_z
                ]


def rows_of(ref, index, block):
    def values():
        rows = ref[(slice(None), *index, slice(block * ROWS, (block + 1) * ROWS))]
        return rows.reshape(rows.shape[0] * ROWS, rows.shape[-1])

    return values


def tap_sums(weights, taps_ref, lane, width, half_z):
    before = taps_ref[:, lane : lane + width]
    here = taps_ref[:, lane + half_z : lane + half_z + width]
    return dot(weights, jnp.concatenate([before, here], axis=0))


def local_kernel(field_ref, weight_ref, acc_ref, taps_ref):
    chans, planes, span_y, span_z = field_ref.shape
    half_z = span_z // 2
    count = span_y // ROWS
    for plane in range(planes):
        blocks = [(rows_of(field_ref, (plane,), b), 0, 8, 1 + 8 * b) for b in range(count)]
        fill_taps(blocks, chans, span_z, taps_ref, plane * 6 * chans)
    taps_ref[:, :half_z] = taps_ref[:, count * 8 * half_z :]
    weights = weight_ref[...]
    width = 8 * half_z
    for step in range(count):
        lane = step * width
        acc_ref[:, lane : lane + width] = tap_sums(weights, taps_ref, lane, width, half_z)


def halo_kernel(part, *refs):
    halo_refs, (weight_ref, acc_ref), part_refs, taps_ref = (
        refs[: part + 1],
        refs[part + 1 : part + 3],
        refs[part + 3 : -1],
        refs[-1],
    )
    chans, _, span_z = halo_refs[0].shape
    half_z = span_z // 2
    lower = halo_refs[0].shape[1] // ROWS - 1
    if part == 0:
        blocks = [(rows_of(halo_refs[0], (), 0), 7, 1, 0)]
        blocks += [(rows_of(halo_refs[0], (), 1 + b), 0, 8, 1 + 8 * b) for b in range(lower)]
    else:
        upper = halo_refs[1].shape[1] // ROWS
        blocks = [(rows_of(halo_refs[0], (), lower), 7, 1, 0)]
        blocks += [(rows_of(halo_refs[1], (), b), 0, 8, 1 + 8 * b) for b in range(upper)]
        blocks += [(rows_of(halo_refs[0], (), 0), 0, 8, 1 + 8 * upper)]
    fill_taps(blocks, chans, span_z, taps_ref, 0)
    weights = weight_ref[...]
    rows = part_refs[0].shape[0]
    count = part_refs[0].shape[1] // half_z
    width = 8 * half_z
    base = part * (acc_ref.shape[1] - count * half_z)
    for step in range(count // 8):
        lane = step * width
        sums = acc_ref[:, base + lane : base + lane + width]
        sums = (sums + tap_sums(weights, taps_ref, lane, width, half_z)).astype(BF16)
        for peer, ref in enumerate(part_refs):
            ref[:, lane : lane + width] = sums[peer * rows : (peer + 1) * rows]


def act_kernel(*refs):
    *part_refs, bias_ref, cot_ref, out_ref, masked_ref = refs
    pre = bias_ref[...] + functools.reduce(
        lambda a, b: a + b, [ref[...].astype(F32) for ref in part_refs]
    )
    small = jnp.exp(-jnp.abs(pre))
    soft = jnp.maximum(pre, 0.0) + jnp.log(1.0 + small)
    out_ref[...] = (0.3 * pre + 0.7 * soft).astype(BF16)
    gate = jnp.where(pre >= 0.0, 1.0, small) / (1.0 + small)
    masked_ref[...] = (cot_ref[...].astype(F32) * (0.3 + 0.7 * gate)).astype(BF16)


def grad_blocks(here, after, weights, blocks, chans, span_z, store):
    half_z = span_z // 2
    size = chans * ROWS
    swap = one_hot((size, size), lambda r, c: c == (r % ROWS) * chans + r // ROWS)
    weave = one_hot((span_z, span_z), lambda m, z: z == 2 * (m % half_z) + m // half_z)
    pair = 2 * chans
    sums = dot(weights, jnp.concatenate(here + after, axis=0))
    beside = []
    for step in range(blocks):
        for parity_x in range(2):
            base = parity_x * 3 * pair
            rows = []
            for j in range(step * 8, step * 8 + 8):
                tile = sums[base : base + 3 * pair, j * half_z : (j + 1) * half_z]
                even = tile[:pair]
                odd = tile[pair : 2 * pair] + pltpu.roll(tile[2 * pair :], half_z - 1, 1)
                rows.append(jnp.concatenate([even.astype(BF16), odd.astype(BF16)], axis=1))
            beside.append(jnp.concatenate(rows, axis=0))
    swapped = dot(swap, jnp.concatenate(beside, axis=1)).astype(BF16)
    below = [swapped[:, i * span_z : (i + 1) * span_z] for i in range(2 * blocks)]
    woven = dot(jnp.concatenate(below, axis=0), weave).astype(BF16)
    for step in range(blocks):
        for parity_x in range(2):
            for chan in range(chans):
                first = (step * 2 + parity_x) * size + chan * ROWS
                store(chan, parity_x, step, woven[first : first + ROWS])


def lanes_of(ref, at, first, last):
    row, lane = at
    return ref[row : row + ROWS, lane + first : lane + last]


def lower_grad_kernel(pieces, *refs):
    *piece_refs, weight_ref, grad_ref = refs
    chans, _, span_y, span_z = grad_ref.shape
    half_z = span_z // 2
    width = span_y // 2 * half_z
    low = [(piece_refs[number], at) for (number, at), _ in pieces]
    here = [lanes_of(*piece, 0, width) for piece in low]
    after = [lanes_of(*piece, half_z, half_z + width) for piece in low]

    def store(chan, parity_x, step, values):
        grad_ref[chan, parity_x, step * ROWS : (step + 1) * ROWS, :] = values

    grad_blocks(here, after, weight_ref[...], span_y // ROWS, chans, span_z, store)


def upper_grad_kernel(pieces, counts, *refs):
    *piece_refs, weight_ref, lower_ref, grad_ref, stage_ref, sems = refs
    chans, _, span_y, span_z = grad_ref.shape
    half_z = span_z // 2
    done = lower_ref.shape[2]
    lower_copy = pltpu.make_async_copy(lower_ref, grad_ref.at[:, :, pl.ds(0, done)], sems.at[0])
    lower_copy.start()
    first, low_end, high_end = done // 2 * half_z, counts[0] * half_z, counts[1] * half_z
    here, after = [], []
    for (low, low_at), (high, high_at) in pieces:
        upper = lanes_of(piece_refs[high], high_at, 0, high_end)
        low_ref = piece_refs[low]
        here.append(jnp.concatenate([lanes_of(low_ref, low_at, first, low_end), upper], axis=1))
        rest = lanes_of(low_ref, low_at, first + half_z, low_end)
        wrapped = lanes_of(low_ref, low_at, 0, half_z)
        after.append(jnp.concatenate([rest, upper, wrapped], axis=1))

    def store(chan, parity_x, step, values):
        stage_ref[chan, parity_x, step * ROWS : (step + 1) * ROWS, :] = values

    grad_blocks(here, after, weight_ref[...], (span_y - done) // ROWS, chans, span_z, store)
    upper_rows = pl.ds(done, span_y - done)
    upper_copy = pltpu.make_async_copy(stage_ref, grad_ref.at[:, :, upper_rows], sems.at[1])
    upper_copy.start()
    lower_copy.wait()
    upper_copy.wait()


def weights_kernel(peers, me_ref, own_ref, local_ref, halo_ref, back_ref):
    _, chans, total = own_ref.shape
    rows = total // peers
    place = ring_place(me_ref[0], peers)

    def tile(tap_x, tap_y, tap_z):
        return own_ref[(tap_x * 3 + tap_y) * 3 + tap_z]

    none = jnp.zeros((chans, total), F32)

    def ahead(r, c):
        return c == ring_device((place + r // rows) % peers, peers) * rows + r % rows

    pick = one_hot((total, total), ahead)
    for ref, taps_x in ((local_ref, (1, 2)), (halo_ref, (0,))):
        tiles = [
            none if tap_y < 0 else tile(tap_x, tap_y, tap_z)
            for taps_y in ((-1, 0), (1, 2))
            for tap_x in taps_x
            for tap_z in range(3)
            for tap_y in taps_y
        ]
        stack = jnp.concatenate(tiles, axis=0).astype(BF16)
        ref[...] = lax.dot_general(
            pick, stack, (((1,), (1,)), ((), ())), preferred_element_type=F32
        ).astype(BF16)

    back = jnp.zeros(back_ref.shape, F32)
    by_offset = ((1, 2), (-1, 0))
    for offset in range(2):
        for plane in range(2):
            tiles = [
                none if min(tap_x, tap_y) < 0 else tile(tap_x, tap_y, tap_z)
                for tap_x in by_offset[plane]
                for tap_z in (1, 2, 0)
                for tap_y in by_offset[offset]
            ]
            stack = jnp.concatenate(tiles, axis=0).astype(BF16)
            first = (offset * 2 + plane) * total

            def behind(r, c, first=first):
                c = c - first
                device = ring_device((place + peers - c // rows) % peers, peers)
                return (r == device * rows + c % rows) & (c >= 0) & (c < total)

            back = back + dot(stack, one_hot((total, 4 * total), behind))
    back_ref[...] = back.astype(BF16)


def call(kernel, name, out_shape, args, scratch=(), flops=0, bytes_accessed=1 << 20, transcendentals=0):
    return pl.pallas_call(
        kernel,
        out_shape=out_shape,
        scratch_shapes=list(scratch),
        compiler_params=PARAMS,
        cost_estimate=pl.CostEstimate(
            flops=flops, bytes_accessed=bytes_accessed, transcendentals=transcendentals
        ),
        name=name,
    )(*args)


def on_device(field, kernel, bias, cotangent):
    peers = lax.axis_size("col")
    me = lax.axis_index("col")
    quarter = peers // 4
    cin, planes, span_y, span_z = field.shape
    cout = bias.shape[0]
    half_y, half_z = span_y // 2, span_z // 2
    counts = (half_y // 2, half_y - half_y // 2)
    starts = (0, counts[0])
    mid = 2 * counts[0]
    last = span_y - ROWS
    plane = lax.optimization_barrier(field[:, planes - 1])
    halos = [jnp.concatenate([plane[:, last:], plane[:, :mid]], axis=1), plane[:, mid:last]]
    halos = [shifted(halo, "gx", 1) for halo in halos]

    chans = -(-cin // 8) * 8
    rows = -(-cout // ROWS) * ROWS
    total = peers * rows
    fill_c = (0, chans - cin)
    fill_o = (0, rows - cout)
    own = lax.dynamic_slice_in_dim(jnp.transpose(kernel, (2, 3, 4, 1, 0)), me * cin, cin, 3)
    own = own.reshape(27, cin, peers, cout)
    own = jnp.pad(own, ((0, 0), fill_c, (0, 0), fill_o)).reshape(27, chans, total)
    own = own.astype(F32)
    field_p = jnp.pad(field, (fill_c, (0, 0), (0, 0), (0, 0)))

    points = half_y * half_z
    vmem = pl.BlockSpec(memory_space=pltpu.VMEM)
    weights_local, weights_halo, weights_back = pl.pallas_call(
        functools.partial(weights_kernel, peers),
        out_shape=[
            jax.ShapeDtypeStruct((total, 24 * chans), BF16),
            jax.ShapeDtypeStruct((total, 12 * chans), BF16),
            jax.ShapeDtypeStruct((12 * chans, 4 * total), BF16),
        ],
        in_specs=[pl.BlockSpec(memory_space=pltpu.SMEM), vmem],
        out_specs=[vmem] * 3,
        compiler_params=PARAMS,
        cost_estimate=pl.CostEstimate(flops=1 << 27, bytes_accessed=1 << 19, transcendentals=0),
        name="weights",
    )(me.astype(jnp.int32).reshape(1), own)
    acc = call(
        local_kernel,
        "local_planes",
        jax.ShapeDtypeStruct((total, points), F32),
        (field_p, weights_local),
        [pltpu.VMEM((planes * 6 * chans, (1 + half_y) * half_z), BF16)],
        flops=2 * total * 24 * chans * points,
        bytes_accessed=1 << 22,
    )
    halos = [jnp.pad(halo, (fill_c, (0, 0), (0, 0))) for halo in halos]
    shapes = [jax.ShapeDtypeStruct((rows, count * half_z), BF16) for count in counts]
    parts = []
    for part in range(2):
        if part:
            weights_halo, parts[0] = lax.optimization_barrier((weights_halo, parts[0]))
        parts.append(
            call(
                functools.partial(halo_kernel, part),
                "halo_plane",
                [shapes[part]] * peers,
                (*halos[: part + 1], weights_halo, acc),
                [pltpu.VMEM((6 * chans, (1 + counts[part]) * half_z), BF16)],
                flops=total * 12 * chans * points,
                bytes_accessed=1 << 21,
            )
        )

    far = 2 * quarter
    steps = (quarter, peers - quarter)
    arrived = [[parts[h][0]] for h in range(2)]
    relayed = [shifted(parts[h][far], "col", steps[h]) for h in range(2)]
    for h in range(2):
        for r in range(1, peers):
            if r not in (steps[h], far):
                sent = parts[h][r]
                if h:
                    sent, relayed[0] = lax.optimization_barrier((sent, relayed[0]))
                arrived[h].append(shifted(sent, "col", r))
    for h in range(2):
        if h:
            relayed[1], arrived[0][-1] = lax.optimization_barrier((relayed[1], arrived[0][-1]))
        joined = (relayed[h].astype(F32) + parts[h][steps[h]].astype(F32)).astype(BF16)
        arrived[h].append(shifted(joined, "col", steps[h]))

    bias_p = [jnp.broadcast_to(jnp.pad(bias, fill_o)[:, None], shape.shape) for shape in shapes]
    cot = jnp.pad(cotangent.reshape(cout, points), (fill_o, (0, 0)))
    acts = [
        call(
            act_kernel,
            "activation",
            (shapes[h], shapes[h]),
            (*arrived[h], bias_p[h], cot[:, starts[h] * half_z : (starts[h] + counts[h]) * half_z]),
            transcendentals=3 * counts[h] * rows * half_z,
        )
        for h in range(2)
    ]
    out = jnp.concatenate([out for out, _ in acts], axis=1)
    out_act = out[:cout].reshape(cout, 1, half_y, half_z)

    masked = [masked for _, masked in acts]
    near = [r for r in range(1, peers) if r != far]
    gathered = [{0: masked[h], **{r: shifted(masked[h], "col", r) for r in near}} for h in range(2)]
    above = [{}, {}]
    arrays = []

    def place_of(value):
        arrays.append(value)
        return len(arrays) - 1

    whole = place_of(shifted(jnp.concatenate(masked, axis=1), "gx", -1))
    for h in range(2):
        above[h][0] = (whole, (0, starts[h] * half_z))
    gathered[0] = lax.optimization_barrier(gathered[0])
    for h in range(2):
        joined = jnp.concatenate([gathered[h][r] for r in near], axis=0)
        number = place_of(shifted(joined, "gx", -1))
        for i, r in enumerate(near):
            above[h][r] = (number, (i * rows, 0))
    for h in range(2):
        gathered[h][far] = shifted(gathered[h][steps[h]], "col", steps[h])
        above[h][far] = (place_of(shifted(gathered[h][far], "gx", -1)), (0, 0))
    mine = [{r: (place_of(gathered[h][r]), (0, 0)) for r in range(peers)} for h in range(2)]
    order = [[places[h][r] for h in range(2)] for places in (mine, above) for r in range(peers)]

    def grad_call(kernel, name, shape, used, extra, blocks):
        used = sorted(used)
        renamed = [[(used.index(n) if n in used else -1, at) for n, at in both] for both in order]
        return call(
            functools.partial(kernel, renamed),
            name,
            shape,
            (*[arrays[n] for n in used], weights_back, *extra),
            flops=8 * total * 12 * chans * 8 * blocks * half_z,
        )

    done = mid - ROWS
    lower = grad_call(
        lower_grad_kernel,
        "lower_grad",
        jax.ShapeDtypeStruct((chans, planes, done, span_z), BF16),
        {both[0][0] for both in order},
        (),
        done // ROWS,
    )
    used = sorted({n for both in order for n, _ in both})
    renamed = [[(used.index(n), at) for n, at in both] for both in order]
    in_grad = pl.pallas_call(
        functools.partial(upper_grad_kernel, renamed, counts),
        out_shape=jax.ShapeDtypeStruct((chans, planes, span_y, span_z), BF16),
        in_specs=[vmem] * (len(used) + 2),
        out_specs=pl.BlockSpec(memory_space=pl.ANY),
        scratch_shapes=[
            pltpu.VMEM((chans, planes, span_y - done, span_z), BF16),
            pltpu.SemaphoreType.DMA((2,)),
        ],
        compiler_params=PARAMS,
        cost_estimate=pl.CostEstimate(
            flops=4 * total * 12 * chans * (span_y - done) * half_z,
            bytes_accessed=1 << 20,
            transcendentals=0,
        ),
        name="upper_grad",
    )(*[arrays[n] for n in used], weights_back, lower)
    return out_act, in_grad[:cin]


def solution(mesh):
    in_specs = (P("col", "gx", None, None), P(), P("col"), P("col", "gx", None, None))
    out_specs = (P("col", "gx", None, None), P("col", "gx", None, None))
    return jax.shard_map(
        on_device, mesh=mesh, in_specs=in_specs, out_specs=out_specs, check_vma=False
    )
```
